32 devices in a mesh: tm: 4 (over y, x), chan: 8 (over z, core).
Axes of the slice: x: 2, y: 2, z: 4, core: 2. Of those that a mesh axis runs over, the one named last changes fastest.
Arguments:
- strain_rate: bfloat16 [20480, 10240], P('tm', 'chan'), may hold values from -120 to 120
- filter_taps: float32 [40], replicated, may hold values from -1 to 1
- send_rows: int32 [32, 4, 8, 32], P(('tm', 'chan')), may hold values from 0 to 319
- pair_source: int32 [32, 2048], P(('tm', 'chan')), may hold values from 0 to 1023, as said below
- pair_receiver: int32 [32, 2048], P(('tm', 'chan')), may hold values from 0 to 319
- pair_count: int32 [32], P(('tm', 'chan')), may hold values from 1024 to 2048, as said below
Outputs:
- correlations: float32 [32, 2048, 256], P(('tm', 'chan'))
The draws below stay inside these ranges and needn't reach their ends.
Inputs may be any that keep to these rules, and one draw needn't show every extreme that they name: `pair_source`: in each owner's list the first 1024 entries name every slot once; the others are any slots. `pair_count`: every owner has at least 1024 live pairs and some owner has exactly 2048.
All inputs are finite; a program needn't handle non-finite values.
Results may differ from the reference program's by a relative error of at most 0.02.
Values may be sent and summed in bfloat16 or wider, within the bound.
No kernel may reach another device: no remote copies, remote signals or barrier semaphores. Data moves between devices by JAX's collectives and lax.ppermute only.
A program may use at most 192 MiB of HBM per device.

```python
import math
import jax
import jax.numpy as jnp
from jax import lax

C = 10240
Q = 5
TAPS = 40
SEG = 1024
NF = 256
WF = 32
F0 = 40
TW = 32
WT = 64
LAGS = 256
SLOTS = 1024
PAIRS = 2048
NT = 20480
NSEG = 4
CH_DEV = 320
OWNERS = 32
CAP = 32
N_TM = 4
N_CHAN = 8


def draw_strain_rate(key, part):
    key = jax.random.fold_in(key, 10)
    key_base, key_scale, key_envelope = jax.random.split(key, 3)
    scales = jnp.exp(jax.random.uniform(key_scale, (C,), jnp.float32, 0.0, math.log(10.0)))
    envelope = jnp.exp(jax.random.uniform(key_envelope, (NT // 40,), jnp.float32, math.log(0.3), math.log(3.0)))
    envelope = jnp.repeat(envelope, 40, total_repeat_length=NT)
    base = jnp.clip(jax.random.normal(key_base, (NT, C), jnp.float32), -4.0, 4.0)
    return (base * envelope[:, None] * scales[None, :]).astype(jnp.bfloat16)


def draw_pair_source(key, part):
    key = jax.random.fold_in(key, 11)
    key_perm, key_rest = jax.random.split(key)
    owner_keys = jax.random.split(key_perm, OWNERS)
    firsts = jax.vmap(lambda owner_key: jax.random.permutation(owner_key, SLOTS))(owner_keys).astype(jnp.int32)
    others = jax.random.randint(key_rest, (OWNERS, PAIRS - SLOTS), 0, SLOTS, dtype=jnp.int32)
    return jnp.concatenate([firsts, others], axis=1)


def draw_pair_count(key, part):
    key = jax.random.fold_in(key, 12)
    key_extra, key_heavy = jax.random.split(key)
    extras = jax.random.randint(key_extra, (3, OWNERS), 0, PAIRS - SLOTS + 1, dtype=jnp.int32)
    counts = SLOTS + jnp.min(extras, axis=0)
    heavy = jax.random.randint(key_heavy, (), 0, OWNERS, dtype=jnp.int32)
    return counts.at[heavy].set(PAIRS).astype(jnp.int32)


def place_ends(values, stream_key, low, high):
    extent = values.shape
    index_at = [jax.random.randint(jax.random.fold_in(stream_key, axis), (), 0, extent[axis]) for axis in range(len(extent))]
    values = values.at[tuple(index_at)].set(low)
    longest = extent.index(max(extent))
    index_at[longest] = (index_at[longest] + 1) % extent[longest]
    return values.at[tuple(index_at)].set(high)


def scatter_about(key, extent, width, most, held_as=jnp.bfloat16):
    return jnp.clip(width * jax.random.normal(key, extent, jnp.float32), -most, most).astype(held_as)


def setup_inputs(seed: int = 0) -> dict:
    key_list = jax.random.split(jax.random.key(seed), 7)
    return {
        "strain_rate": draw_strain_rate(jax.random.fold_in(key_list[6], 71), 0),
        "filter_taps": scatter_about(key_list[1], (TAPS,), TAPS ** -0.5, 1.0, jnp.float32),
        "send_rows": place_ends(jax.random.randint(key_list[2], (OWNERS, N_TM, N_CHAN, CAP), 0, CH_DEV), jax.random.fold_in(key_list[2], 1), 0, CH_DEV - 1).astype(jnp.int32),
        "pair_source": draw_pair_source(jax.random.fold_in(key_list[6], 71), 0),
        "pair_receiver": place_ends(jax.random.randint(key_list[4], (OWNERS, PAIRS), 0, CH_DEV), jax.random.fold_in(key_list[4], 1), 0, CH_DEV - 1).astype(jnp.int32),
        "pair_count": draw_pair_count(jax.random.fold_in(key_list[6], 71), 0),
    }


def decimate(padded, filter_taps, out_length, axis):
    summed = None
    for offset in range(TAPS):
        strided = lax.slice_in_dim(padded, offset, offset + Q * (out_length - 1) + 1, Q, axis)
        tap_term = filter_taps[offset] * strided.astype(jnp.float32)
        summed = tap_term if offset == 0 else summed + tap_term
    return summed.astype(jnp.bfloat16)

def forward_table():
    sample_ids = jnp.arange(SEG, dtype=jnp.int32)[:, None]
    bin_ids = (F0 - WF + jnp.arange(NF + 2 * WF, dtype=jnp.int32))[None, :]
    phases = (sample_ids * bin_ids % SEG).astype(jnp.float32) * (2.0 * math.pi / SEG)
    return jnp.concatenate([jnp.cos(phases), -jnp.sin(phases)], axis=1).astype(jnp.bfloat16)

def lag_table():
    bin_ids = (F0 + jnp.arange(NF, dtype=jnp.int32))[:, None]
    lag_ids = (jnp.arange(LAGS, dtype=jnp.int32) - LAGS // 2)[None, :]
    phases = (bin_ids * lag_ids % SEG).astype(jnp.float32) * (2.0 * math.pi / SEG)
    return jnp.concatenate([jnp.cos(phases), -jnp.sin(phases)], axis=0).astype(jnp.bfloat16)

def taper():
    bin_ids = jnp.arange(NF, dtype=jnp.int32)
    edge_dist = jnp.minimum(bin_ids, NF - 1 - bin_ids).astype(jnp.float32)
    return jnp.where(edge_dist < TW, 0.5 - 0.5 * jnp.cos(math.pi * (edge_dist + 0.5) / TW), 1.0)

def whiten(decimated):
    signal = decimated.astype(jnp.float32)
    length = signal.shape[1]
    window = lax.reduce_window(jnp.abs(signal), jnp.asarray(0.0, signal.dtype), lax.add, (1, 2 * WT + 1), (1, 1), ((0, 0), (WT, WT)))
    sample_ids = jnp.arange(length, dtype=jnp.int32)
    counts = (jnp.minimum(sample_ids + WT, length - 1) - jnp.maximum(sample_ids - WT, 0) + 1).astype(signal.dtype)
    flattened = (signal / (window / counts + 1e-05)).astype(jnp.bfloat16)
    segments = length // SEG
    pieces = flattened.reshape(-1, SEG)
    spectrum = jnp.dot(pieces, forward_table(), preferred_element_type=jnp.float32)
    bins_kept = NF + 2 * WF
    real_part = spectrum[:, :bins_kept]
    imag_part = spectrum[:, bins_kept:]
    magnitude = jnp.sqrt(real_part * real_part + imag_part * imag_part)
    smooth = lax.reduce_window(magnitude, jnp.asarray(0.0, magnitude.dtype), lax.add, (1, 2 * WF + 1), (1, 1), 'VALID') / (2 * WF + 1)
    factor = taper()[None, :] / (smooth + 1e-05)
    whitened = jnp.concatenate([real_part[:, WF:WF + NF] * factor, imag_part[:, WF:WF + NF] * factor], axis=1)
    return whitened.astype(jnp.bfloat16).reshape(signal.shape[0], segments, 2 * NF)

def correlate(source_rows, receiver_rows):
    source = source_rows.astype(jnp.float32)
    receiver = receiver_rows.astype(jnp.float32)
    cross_real = lax.optimization_barrier(jnp.sum(source[..., :NF] * receiver[..., :NF] + source[..., NF:] * receiver[..., NF:], axis=1))
    cross_imag = lax.optimization_barrier(jnp.sum(source[..., NF:] * receiver[..., :NF] - source[..., :NF] * receiver[..., NF:], axis=1))
    cross_all = jnp.concatenate([cross_real, cross_imag], axis=1).astype(jnp.bfloat16)
    norm_scale = 1.0 / math.sqrt(source_rows.shape[1] * NF)
    return jnp.dot(cross_all, lag_table(), preferred_element_type=jnp.float32) * norm_scale

def reference(strain_rate, filter_taps, send_rows, pair_source, pair_receiver, pair_count):
    rim_width = TAPS // 2

    def prepare(group_id):
        series = lax.dynamic_slice_in_dim(strain_rate, group_id * CH_DEV, CH_DEV, 1)
        padded = jnp.pad(series, ((rim_width, rim_width), (0, 0)))
        decimated = decimate(padded, filter_taps, series.shape[0] // Q, 0)
        return whiten(decimated.T)
    whitened_all = lax.map(prepare, jnp.arange(C // CH_DEV, dtype=jnp.int32)).reshape(C, NSEG, 2 * NF)
    chan_width = C // N_CHAN

    def channel_of(device, local_ids):
        return device % N_CHAN * chan_width + device // N_CHAN * CH_DEV + local_ids

    def per_owner(owner_id):
        slot_ids = pair_source[owner_id]
        sender = slot_ids // CAP
        column = slot_ids % CAP
        local_ids = send_rows[sender, owner_id // N_CHAN, owner_id % N_CHAN, column]
        source_ids = channel_of(sender, local_ids)
        receiver_ids = channel_of(owner_id, pair_receiver[owner_id])
        values = correlate(whitened_all[source_ids], whitened_all[receiver_ids])
        places = jnp.arange(PAIRS, dtype=jnp.int32)
        return jnp.where((places < pair_count[owner_id])[:, None], values, 0.0)
    return lax.map(per_owner, jnp.arange(N_TM * N_CHAN, dtype=jnp.int32))
```

```python
import math

import jax
import jax.numpy as jnp
import numpy as np
from jax import lax
from jax.experimental import pallas as pl
from jax.experimental.pallas import tpu as pltpu
from jax.sharding import PartitionSpec as P

Q = 5
TAPS = 40
RIM = TAPS // 2
SEG = 1024
NF = 256
WF = 32
F0 = 40
TW = 32
WT = 64
LAGS = 256
BINS = NF + 2 * WF
TB = 128
EDGE = 32
BAND = 704
FIRST = 672
BF = jnp.bfloat16
F32 = jnp.float32
VMEM = 56 * 1024 * 1024


def forward_table():
    phases = np.arange(F0 - WF, F0 + NF + WF)[:, None] * np.arange(SEG)[None, :] % SEG
    phases = phases * (2.0 * np.pi / SEG)
    return np.concatenate([np.cos(phases), -np.sin(phases)], axis=0).astype(BF)


def lag_table():
    phases = (F0 + np.arange(NF))[:, None] * (np.arange(LAGS) - LAGS // 2)[None, :] % SEG
    phases = phases * (2.0 * np.pi / SEG)
    return np.concatenate([np.cos(phases), -np.sin(phases)], axis=0).astype(BF)


def taper():
    bins = np.arange(NF)
    edge = np.minimum(bins, NF - 1 - bins)
    return np.where(edge < TW, 0.5 - 0.5 * np.cos(np.pi * (edge + 0.5) / TW), 1.0).astype(np.float32)


def ones_band(rows, columns, width):
    lag = np.arange(columns)[None, :] - np.arange(rows)[:, None]
    return ((lag >= 0) & (lag < width)).astype(BF)


def whole(shape):
    return pl.BlockSpec(shape, lambda *_: (0,) * len(shape))


def params():
    return pltpu.CompilerParams(vmem_limit_bytes=VMEM)


def band_kernel(taps_ref, main_ref, first_ref, last_ref):
    def fill(ref, start):
        width = ref.shape[1]
        tap = (
            lax.broadcasted_iota(jnp.int32, (TB, width), 1)
            + (start + RIM)
            - Q * lax.broadcasted_iota(jnp.int32, (TB, width), 0)
        )
        values = jnp.zeros((TB, width), F32)
        for k in range(TAPS):
            values = jnp.where(tap == k, taps_ref[k], values)
        upper = values.astype(BF)
        ref[:TB] = upper
        ref[TB:] = (values - upper.astype(F32)).astype(BF)

    fill(main_ref, -EDGE)
    fill(first_ref, 0)
    fill(last_ref, Q * TB)


def filter_bands(taps):
    widths = (BAND, FIRST, EDGE)
    return pl.pallas_call(
        band_kernel,
        in_specs=[pl.BlockSpec(memory_space=pltpu.SMEM)],
        out_shape=[jax.ShapeDtypeStruct((2 * TB, width), BF) for width in widths],
        compiler_params=params(),
    )(taps)


def decimate_kernel(x_ref, rim_ref, main_ref, first_ref, last_ref, out_ref):
    blocks = out_ref.shape[0] // TB
    for b in range(blocks):
        start = Q * TB * b
        if b == 0:
            total = jnp.dot(first_ref[...], x_ref[:FIRST], preferred_element_type=F32)
            total += jnp.dot(main_ref[:, :EDGE], rim_ref[:EDGE], preferred_element_type=F32)
        elif b < blocks - 1:
            total = jnp.dot(
                main_ref[...], x_ref[start - EDGE : start - EDGE + BAND], preferred_element_type=F32
            )
        else:
            width = EDGE + Q * TB
            total = jnp.dot(
                main_ref[:, :width], x_ref[start - EDGE :], preferred_element_type=F32
            )
            total += jnp.dot(last_ref[...], rim_ref[EDGE:], preferred_element_type=F32)
        out_ref[TB * b : TB * (b + 1)] = (total[:TB] + total[TB:]).astype(BF)


def lane_chunk(width):
    return 256 if width % 256 == 0 else 128


def decimate(x, rim, bands):
    rows, width = x.shape
    chunk = lane_chunk(width)
    return pl.pallas_call(
        decimate_kernel,
        grid=(width // chunk,),
        in_specs=[
            pl.BlockSpec((rows, chunk), lambda c: (0, c)),
            pl.BlockSpec((2 * EDGE, chunk), lambda c: (0, c)),
        ]
        + [whole(band.shape) for band in bands],
        out_specs=pl.BlockSpec((rows // Q, chunk), lambda c: (0, c)),
        out_shape=jax.ShapeDtypeStruct((rows // Q, width), BF),
        compiler_params=params(),
    )(x, rim, *bands)


def whiten_kernel(
    place_ref, dec_ref, before_ref, after_ref, ones_ref, table_ref, smooth_ref, taper_ref, out_ref, size, flat
):
    length = dec_ref.shape[0]
    blocks = length // TB
    size[:WT] = jnp.abs(before_ref[...])
    size[WT : WT + length] = jnp.abs(dec_ref[...])
    size[WT + length :] = jnp.abs(after_ref[...])
    origin = place_ref[0] * length
    total = place_ref[1] * length
    for b in range(blocks):
        window = jnp.dot(ones_ref[...], size[TB * b : TB * b + TB + 2 * WT], preferred_element_type=F32)
        if b == 0 or b == blocks - 1:
            place = origin + TB * b + lax.broadcasted_iota(jnp.int32, (TB, 1), 0)
            count = jnp.minimum(place + WT, total - 1) - jnp.maximum(place - WT, 0) + 1
            mean = window / count.astype(F32)
        else:
            mean = window * (1.0 / (2 * WT + 1))
        values = dec_ref[TB * b : TB * (b + 1)].astype(F32) / (mean + 1e-05)
        flat[TB * b : TB * (b + 1)] = values.astype(BF)
    spectrum = jnp.dot(table_ref[...], flat[...], preferred_element_type=F32)
    real, imag = spectrum[:BINS], spectrum[BINS:]
    magnitude = jnp.sqrt(real * real + imag * imag)
    upper = magnitude.astype(BF)
    lower = (magnitude - upper.astype(F32)).astype(BF)
    smooth = jnp.dot(smooth_ref[...], upper, preferred_element_type=F32)
    smooth += jnp.dot(smooth_ref[...], lower, preferred_element_type=F32)
    factor = taper_ref[...] / (smooth * (1.0 / (2 * WF + 1)) + 1e-05)
    out_ref[:, :NF] = (real[WF : WF + NF] * factor).T.astype(BF)
    out_ref[:, NF:] = (imag[WF : WF + NF] * factor).T.astype(BF)


def whiten(place, dec, before, after):
    length, width = dec.shape
    chunk = lane_chunk(width)
    tables = (
        ones_band(TB, TB + 2 * WT, 2 * WT + 1),
        forward_table(),
        ones_band(NF, BINS, 2 * WF + 1),
        taper()[:, None],
    )
    column = lambda c: (0, c)
    return pl.pallas_call(
        whiten_kernel,
        grid=(width // chunk,),
        in_specs=[
            pl.BlockSpec(memory_space=pltpu.SMEM),
            pl.BlockSpec((length, chunk), column),
            pl.BlockSpec((WT, chunk), column),
            pl.BlockSpec((WT, chunk), column),
        ]
        + [whole(table.shape) for table in tables],
        out_specs=pl.BlockSpec((chunk, 2 * NF), lambda c: (c, 0)),
        out_shape=jax.ShapeDtypeStruct((width, 2 * NF), BF),
        scratch_shapes=[pltpu.VMEM((length + 2 * WT, chunk), BF), pltpu.VMEM((length, chunk), BF)],
        compiler_params=params(),
    )(place, dec, before, after, *tables)


def one_hot(ids, columns):
    hits = ids == lax.broadcasted_iota(jnp.int32, (ids.shape[0], columns), 1)
    return jnp.where(hits, 1.0, 0.0).astype(BF)


def pick_kernel(ids_ref, rows_ref, out_ref):
    owners, rows, width = out_ref.shape
    picked = jnp.dot(one_hot(ids_ref[...], rows_ref.shape[0]), rows_ref[...], preferred_element_type=F32)
    out_ref[...] = picked.astype(BF).reshape(owners, rows, width)


def pick(ids, spectra, owners, groups, capacity):
    join = 1
    while join * capacity % 16 != 0:
        join *= 2
    steps = groups // join
    held = spectra.shape[0] // steps
    local = ids.reshape(steps, join, owners, capacity).transpose(0, 2, 1, 3)
    local = local + (jnp.arange(join, dtype=jnp.int32) * (held // join))[None, None, :, None]
    rows = owners * join * capacity
    return pl.pallas_call(
        pick_kernel,
        grid=(steps,),
        in_specs=[
            pl.BlockSpec((rows, 1), lambda g: (g, 0)),
            pl.BlockSpec((held, 2 * NF), lambda g: (g, 0)),
        ],
        out_specs=pl.BlockSpec((owners, join * capacity, 2 * NF), lambda g: (0, g, 0)),
        out_shape=jax.ShapeDtypeStruct((owners, groups * capacity, 2 * NF), BF),
        compiler_params=params(),
    )(local.reshape(steps * rows, 1), spectra)


def correlate_kernel(count_ref, ids_ref, source_ref, receiver_ref, table_ref, out_ref):
    pairs = out_ref.shape[0]
    segments = source_ref.shape[0]
    pick_source = one_hot(ids_ref[:, :1], source_ref.shape[1])
    pick_receiver = one_hot(ids_ref[:, 1:], receiver_ref.shape[1])
    real = imag = None
    for s in range(segments):
        a = jnp.dot(pick_source, source_ref[s], preferred_element_type=F32)
        b = jnp.dot(pick_receiver, receiver_ref[s], preferred_element_type=F32)
        a_re, a_im, b_re, b_im = a[:, :NF], a[:, NF:], b[:, :NF], b[:, NF:]
        re = a_re * b_re + a_im * b_im
        im = a_im * b_re - a_re * b_im
        real = re if s == 0 else real + re
        imag = im if s == 0 else imag + im
    values = jnp.dot(real.astype(BF), table_ref[:NF], preferred_element_type=F32)
    values += jnp.dot(imag.astype(BF), table_ref[NF:], preferred_element_type=F32)
    place = pl.program_id(0) * pairs + lax.broadcasted_iota(jnp.int32, values.shape, 0)
    scale = 1.0 / math.sqrt(segments * NF)
    out_ref[...] = jnp.where(place < count_ref[0], values * scale, 0.0)


def correlate(count, ids, source, receiver):
    pairs = ids.shape[0]
    block = 256
    return pl.pallas_call(
        correlate_kernel,
        grid=(pairs // block,),
        in_specs=[
            pl.BlockSpec(memory_space=pltpu.SMEM),
            pl.BlockSpec((block, 2), lambda p: (p, 0)),
            whole(source.shape),
            whole(receiver.shape),
            whole((2 * NF, LAGS)),
        ],
        out_specs=pl.BlockSpec((block, LAGS), lambda p: (p, 0)),
        out_shape=jax.ShapeDtypeStruct((pairs, LAGS), F32),
        compiler_params=params(),
    )(count, ids, source, receiver, lag_table())


def from_neighbours(low, high):
    count = lax.axis_size("tm")
    before = lax.ppermute(high, "tm", [(i, i + 1) for i in range(count - 1)])
    after = lax.ppermute(low, "tm", [(i + 1, i) for i in range(count - 1)])
    return before, after


def on_device(strain, taps, send_rows, pair_source, pair_receiver, pair_count):
    n_tm, n_chan = lax.axis_size("tm"), lax.axis_size("chan")
    owners = n_tm * n_chan
    capacity = send_rows.shape[3]
    before, after = from_neighbours(strain[:EDGE], strain[-EDGE:])
    bands = filter_bands(taps)
    asked = lax.all_gather(send_rows[0], "tm")
    dec = decimate(strain, jnp.concatenate([before, after]), bands)
    before, after = from_neighbours(dec[:WT], dec[-WT:])
    place = jnp.stack([lax.axis_index("tm"), jnp.int32(n_tm)]).astype(jnp.int32)
    spectra = whiten(place, dec, before, after)
    outgoing = pick(asked.reshape(-1), spectra, owners, n_tm, capacity)
    source = lax.all_to_all(outgoing, ("tm", "chan"), 0, 0, tiled=True)
    source = source.reshape(n_tm, -1, 2 * NF)
    receiver = lax.all_to_all(spectra.reshape(n_tm, -1, 2 * NF), "tm", 0, 0, tiled=True)
    sender, column = pair_source[0] // capacity, pair_source[0] % capacity
    slot = (sender % n_chan * n_tm + sender // n_chan) * capacity + column
    ids = jnp.stack([slot, pair_receiver[0]], axis=1)
    return correlate(pair_count, ids, source, receiver)[None]


def solution(mesh):
    return jax.shard_map(
        on_device,
        mesh=mesh,
        in_specs=(
            P("tm", "chan"),
            P(),
            P(("tm", "chan"), None, None, None),
            P(("tm", "chan"), None),
            P(("tm", "chan"), None),
            P(("tm", "chan")),
        ),
        out_specs=P(("tm", "chan"), None, None),
        check_vma=False,
    )
```

```python
import functools
import math

import jax
import jax.numpy as jnp
import numpy as np
from jax import lax
from jax.experimental import pallas as pl
from jax.experimental.pallas import tpu as pltpu
from jax.sharding import Mesh
from jax.sharding import PartitionSpec as P

Q = 5
TAPS = 40
RIM = TAPS // 2
SEG = 1024
NF = 256
WF = 32
F0 = 40
TW = 32
WT = 64
LAGS = 256
BINS = NF + 2 * WF
TB = 128
RAW = 64
LEAD = 32
BAND = 704
NH = NF // 2
BF = jnp.bfloat16
F32 = jnp.float32
VMEM = 56 * 1024 * 1024


def forward_table():
    phases = np.arange(F0 - WF, F0 + NF + WF)[:, None] * np.arange(SEG)[None, :] % SEG
    phases = phases * (2.0 * np.pi / SEG)
    return np.concatenate([np.cos(phases), -np.sin(phases)], axis=0).astype(BF)


def lag_table():
    phases = (F0 + np.arange(NF))[:, None] * (np.arange(LAGS) - LAGS // 2)[None, :] % SEG
    phases = phases * (2.0 * np.pi / SEG)
    return np.concatenate([np.cos(phases), -np.sin(phases)], axis=0).astype(BF)


def taper():
    bins = np.arange(NF)
    edge = np.minimum(bins, NF - 1 - bins)
    return np.where(edge < TW, 0.5 - 0.5 * np.cos(np.pi * (edge + 0.5) / TW), 1.0).astype(np.float32)


def ones_band(rows, columns, width):
    lag = np.arange(columns)[None, :] - np.arange(rows)[:, None]
    return ((lag >= 0) & (lag < width)).astype(BF)


def whole(shape):
    return pl.BlockSpec(shape, lambda *_: (0,) * len(shape))


def params():
    return pltpu.CompilerParams(vmem_limit_bytes=VMEM)


def fill_band(band_ref, taps_ref, work_ref, rows, shift):
    lanes = work_ref.shape[1]
    tap = lax.broadcasted_iota(jnp.int32, (8, 128), 1) - Q * lax.broadcasted_iota(jnp.int32, (8, 128), 0)
    pattern = jnp.zeros((8, 128), F32)
    for k in range(TAPS):
        pattern = jnp.where(tap == k, taps_ref[k], pattern)
    pattern = jnp.concatenate([pattern, jnp.zeros((8, lanes - 128), F32)], axis=1)
    for m in range(0, rows, 8):
        work_ref[m : m + 8] = pltpu.roll(pattern, (Q * m + shift) % lanes, 1)
    values = work_ref[:rows, : band_ref.shape[1]]
    upper = values.astype(BF)
    band_ref[:rows] = upper
    band_ref[rows:] = (values - upper.astype(F32)).astype(BF)


def filtered(band, x):
    both = jnp.dot(band, x, preferred_element_type=F32)
    rows = both.shape[0] // 2
    return (both[:rows] + both[rows:]).astype(BF)


EDGE_ROWS = 512
EDGE_READ = 352


def edge_kernel(taps_ref, first_ref, last_ref, low_ref, high_ref, fix_ref, low_band, high_band, work):
    fill_band(low_band, taps_ref, work, WT, -RIM)
    fill_band(high_band, taps_ref, work, WT, EDGE_READ - Q * WT - RIM)
    fill_band(fix_ref, taps_ref, work, 16, RAW - Q * 8 - RIM)
    low_ref[:RAW] = first_ref[:RAW]
    low_ref[RAW:] = filtered(low_band[...], first_ref[:EDGE_READ])
    high_ref[:RAW] = last_ref[EDGE_ROWS - RAW :]
    high_ref[RAW:] = filtered(high_band[...], last_ref[EDGE_ROWS - EDGE_READ :])


def edges(x, taps):
    rows, width = x.shape
    last = rows // EDGE_ROWS - 1
    return pl.pallas_call(
        edge_kernel,
        grid=(1,),
        in_specs=[
            pl.BlockSpec(memory_space=pltpu.SMEM),
            pl.BlockSpec((EDGE_ROWS, width), lambda c: (0, 0)),
            pl.BlockSpec((EDGE_ROWS, width), lambda c: (last, 0)),
        ],
        out_specs=[whole((RAW + WT, width)), whole((RAW + WT, width)), whole((32, 2 * RAW))],
        out_shape=[
            jax.ShapeDtypeStruct((RAW + WT, width), BF),
            jax.ShapeDtypeStruct((RAW + WT, width), BF),
            jax.ShapeDtypeStruct((32, 2 * RAW), BF),
        ],
        scratch_shapes=[
            pltpu.VMEM((2 * WT, EDGE_READ), BF),
            pltpu.VMEM((2 * WT, EDGE_READ), BF),
            pltpu.VMEM((WT, 512), F32),
        ],
        compiler_params=params(),
    )(taps, x, x)


def decimate_kernel(taps_ref, x_ref, out_ref, main, first, work):
    @pl.when(pl.program_id(0) == 0)
    def _():
        fill_band(main, taps_ref, work, TB, LEAD - RIM)
        fill_band(first, taps_ref, work, TB, -RIM)

    blocks = out_ref.shape[0] // TB
    for b in range(blocks):
        if b == 0:
            band, rows = first[...], x_ref[: BAND - LEAD]
        elif b < blocks - 1:
            band, rows = main[...], x_ref[Q * TB * b - LEAD : Q * TB * b - LEAD + BAND]
        else:
            band, rows = main[:, : LEAD + Q * TB], x_ref[Q * TB * b - LEAD :]
        out_ref[TB * b : TB * (b + 1)] = filtered(band, rows)


def lane_chunk(width):
    return next(chunk for chunk in (256, 640, 128) if width % chunk == 0)


def decimate(x, taps):
    rows, width = x.shape
    chunk = lane_chunk(width)
    return pl.pallas_call(
        decimate_kernel,
        grid=(width // chunk,),
        in_specs=[
            pl.BlockSpec(memory_space=pltpu.SMEM),
            pl.BlockSpec((rows, chunk), lambda c: (0, c)),
        ],
        out_specs=pl.BlockSpec((rows // Q, chunk), lambda c: (0, c)),
        out_shape=jax.ShapeDtypeStruct((rows // Q, width), BF),
        scratch_shapes=[
            pltpu.VMEM((2 * TB, BAND), BF),
            pltpu.VMEM((2 * TB, BAND - LEAD), BF),
            pltpu.VMEM((TB, 768), F32),
        ],
        compiler_params=params(),
    )(taps, x)


def inverse(values):
    guess = pl.reciprocal(values, approx=True)
    return guess * (2.0 - values * guess)


def whiten_kernel(
    place_ref, dec_ref, first_ref, last_ref, before_ref, after_ref, fix_ref, ones_ref, table_ref, smooth_ref,
    taper_ref, low_ref, high_ref, size, flat
):
    length = dec_ref.shape[0]
    blocks = length // TB
    place, count = place_ref[0], place_ref[1]
    low = filtered(fix_ref[...], jnp.concatenate([before_ref[:RAW], first_ref[...]])).astype(F32)
    high = filtered(fix_ref[...], jnp.concatenate([last_ref[...], after_ref[:RAW]])).astype(F32)
    before = jnp.concatenate([before_ref[RAW:].astype(F32)[:-8], low[:8]])
    after = jnp.concatenate([high[8:], after_ref[RAW:].astype(F32)[8:]])
    size[:WT] = jnp.abs(jnp.where(place > 0, before, 0.0)).astype(BF)
    size[WT + length :] = jnp.abs(jnp.where(place < count - 1, after, 0.0)).astype(BF)
    flat[...] = dec_ref[...]
    flat[:TB] = jnp.concatenate([low[8:], dec_ref[:TB].astype(F32)[8:]]).astype(BF)
    flat[length - TB :] = jnp.concatenate([dec_ref[length - TB :].astype(F32)[:-8], high[:8]]).astype(BF)
    size[WT : WT + length] = jnp.abs(flat[...])
    for b in range(blocks):
        mean = jnp.dot(ones_ref[...], size[TB * b : TB * b + TB + 2 * WT], preferred_element_type=F32)
        if b == 0 or b == blocks - 1:
            sample = place * length + TB * b + lax.broadcasted_iota(jnp.int32, (TB, 1), 0)
            total = jnp.minimum(sample + WT, count * length - 1) - jnp.maximum(sample - WT, 0) + 1
            mean = mean / total.astype(F32)
        else:
            mean = mean * (1.0 / (2 * WT + 1))
        rows = slice(TB * b, TB * (b + 1))
        flat[rows] = (flat[rows].astype(F32) * inverse(mean + 1e-05)).astype(BF)
    spectrum = jnp.dot(table_ref[...], flat[...], preferred_element_type=F32)
    real, imag = spectrum[:BINS], spectrum[BINS:]
    magnitude = jnp.sqrt(real * real + imag * imag)
    upper = magnitude.astype(BF)
    lower = (magnitude - upper.astype(F32)).astype(BF)
    smooth = jnp.dot(smooth_ref[...], upper, preferred_element_type=F32)
    smooth += jnp.dot(smooth_ref[...], lower, preferred_element_type=F32)
    factor = taper_ref[...] * inverse(smooth * (1.0 / (2 * WF + 1)) + 1e-05)
    real, imag = real[WF : WF + NF] * factor, imag[WF : WF + NF] * factor
    low_ref[:, :NH] = real[:NH].T.astype(BF)
    low_ref[:, NH:] = imag[:NH].T.astype(BF)
    high_ref[:, :NH] = real[NH:].T.astype(BF)
    high_ref[:, NH:] = imag[NH:].T.astype(BF)


def whiten(place, dec, x, before, after, fix, part, parts):
    rows, width = x.shape
    length = dec.shape[0]
    held = width // parts
    chunk = lane_chunk(held)
    steps = held // chunk
    first = part * steps
    tables = (
        ones_band(TB, TB + 2 * WT, 2 * WT + 1),
        forward_table(),
        ones_band(NF, BINS, 2 * WF + 1),
        taper()[:, None],
    )
    column = lambda c: (0, first + c)
    last = rows // RAW - 1
    return pl.pallas_call(
        whiten_kernel,
        grid=(steps,),
        in_specs=[
            pl.BlockSpec(memory_space=pltpu.SMEM),
            pl.BlockSpec((length, chunk), column),
            pl.BlockSpec((RAW, chunk), column),
            pl.BlockSpec((RAW, chunk), lambda c: (last, first + c)),
            pl.BlockSpec((RAW + WT, chunk), column),
            pl.BlockSpec((RAW + WT, chunk), column),
            whole(fix.shape),
        ]
        + [whole(table.shape) for table in tables],
        out_specs=[pl.BlockSpec((chunk, 2 * NH), lambda c: (c, 0))] * 2,
        out_shape=[jax.ShapeDtypeStruct((held, 2 * NH), BF)] * 2,
        scratch_shapes=[pltpu.VMEM((length + 2 * WT, chunk), BF), pltpu.VMEM((length, chunk), BF)],
        compiler_params=params(),
    )(place, dec, x, x, before, after, fix, *tables)


def one_hot(ids, columns):
    hits = ids == lax.broadcasted_iota(jnp.int32, (ids.shape[0], columns), 1)
    return jnp.where(hits, 1.0, 0.0).astype(BF)


def pick_kernel(each, ids_ref, *refs):
    out_ref = refs[-1]
    owners, rows, _ = out_ref.shape
    parts = refs[:-1]
    step = pl.program_id(0)
    for p in range(len(parts) // (out_ref.shape[2] // (2 * NH))):
        halves = parts[p :: len(parts) // (out_ref.shape[2] // (2 * NH))]

        @pl.when(step // each == p)
        def _(halves=halves):
            hot = one_hot(ids_ref[...], halves[0].shape[0])
            for h, ref in enumerate(halves):
                picked = jnp.dot(hot, ref[...], preferred_element_type=F32)
                out_ref[:, :, 2 * NH * h : 2 * NH * (h + 1)] = picked.astype(BF).reshape(owners, rows, 2 * NH)


def pick(ids, halves):
    groups, owners, capacity = ids.shape
    parts = len(halves[0])
    held_all = parts * halves[0][0].shape[0]
    join = 1
    while join * capacity % 16 != 0:
        join *= 2
    steps = groups // join
    each = steps // parts
    held = held_all // steps
    local = ids.reshape(steps, join, owners, capacity).transpose(0, 2, 1, 3)
    local = local + (jnp.arange(join, dtype=jnp.int32) * (held // join))[None, None, :, None]
    rows = owners * join * capacity
    specs = [
        pl.BlockSpec((held, 2 * NH), lambda g, p=p: (jnp.clip(g - p * each, 0, each - 1), 0))
        for _ in halves
        for p in range(parts)
    ]
    return pl.pallas_call(
        functools.partial(pick_kernel, each),
        grid=(steps,),
        in_specs=[pl.BlockSpec((rows, 1), lambda g: (g, 0))] + specs,
        out_specs=pl.BlockSpec((owners, join * capacity, 2 * NH * len(halves)), lambda g: (0, g, 0)),
        out_shape=jax.ShapeDtypeStruct((owners, groups * capacity, 2 * NH * len(halves)), BF),
        compiler_params=params(),
    )(local.reshape(steps * rows, 1), *[part for half in halves for part in half])


def correlate_kernel(segments, scalar_ref, ids_ref, own_ref, mirrored_ref, table_ref, *refs):
    receivers, rest = refs[:segments], refs[segments:]
    out_ref = rest[-1]
    pairs = out_ref.shape[0]
    held = own_ref.shape[1]
    slots = ids_ref[:, :1]
    pick_own = one_hot(slots, held)
    pick_mirrored = one_hot(slots - held, held)
    pick_receiver = one_hot(ids_ref[:, 1:], receivers[0].shape[0])
    real = imag = None
    for k in range(segments):
        s = scalar_ref[1 + k]
        a = jnp.dot(pick_own, own_ref[s], preferred_element_type=F32)
        a += jnp.dot(pick_mirrored, mirrored_ref[s], preferred_element_type=F32)
        b = jnp.dot(pick_receiver, receivers[k][...], preferred_element_type=F32)
        a_re, a_im, b_re, b_im = a[:, :NH], a[:, NH:], b[:, :NH], b[:, NH:]
        re = a_re * b_re + a_im * b_im
        im = a_im * b_re - a_re * b_im
        real = re if k == 0 else real + re
        imag = im if k == 0 else imag + im
    values = jnp.dot(real.astype(BF), table_ref[:NH], preferred_element_type=F32)
    values += jnp.dot(imag.astype(BF), table_ref[NH:], preferred_element_type=F32)
    if len(rest) == 1:
        out_ref[...] = values
    else:
        place = pl.program_id(0) * pairs + lax.broadcasted_iota(jnp.int32, values.shape, 0)
        scale = 1.0 / math.sqrt(segments * NF)
        out_ref[...] = jnp.where(place < scalar_ref[0], (rest[0][...] + values) * scale, 0.0)


def correlate(scalars, ids, own, mirrored, receivers, half, partial):
    pairs = ids.shape[0]
    segments = len(receivers)
    block = min(pairs, 1024)
    table = lag_table().reshape(2, 2, NH, LAGS)[:, half].reshape(2 * NH, LAGS)
    once = pl.Buffered(1)
    row = pl.BlockSpec((block, LAGS), lambda p: (p, 0))
    lanes = lambda p: (0, half)
    return pl.pallas_call(
        functools.partial(correlate_kernel, segments),
        grid=(pairs // block,),
        in_specs=[
            pl.BlockSpec(memory_space=pltpu.SMEM),
            pl.BlockSpec((block, 2), lambda p: (p, 0)),
            pl.BlockSpec(own.shape[:2] + (2 * NH,), lambda p: (0, 0, half), pipeline_mode=once),
            pl.BlockSpec(mirrored.shape, lambda p: (0, 0, 0), pipeline_mode=once),
            whole(table.shape),
        ]
        + [pl.BlockSpec((r.shape[0], 2 * NH), lanes, pipeline_mode=once) for r in receivers]
        + [row for _ in partial],
        out_specs=row,
        out_shape=jax.ShapeDtypeStruct((pairs, LAGS), F32),
        compiler_params=params(),
    )(scalars, ids, own, mirrored, table, *receivers, *partial)


def on_device(strain, taps, send_rows, pair_source, pair_receiver, pair_count):
    n_tm, n_sub = lax.axis_size("tm"), lax.axis_size("sub")
    my_tm, my_half = lax.axis_index("tm"), lax.axis_index("half")
    capacity = send_rows.shape[3]
    width = strain.shape[1]
    parts = 2 if width % 256 == 0 and n_tm % 2 == 0 and width // 2 % 128 == 0 else 1
    swap = [(0, 1), (1, 0)]

    def shifted(array, by):
        return lax.ppermute(array, "tm", [(i, (i + by) % n_tm) for i in range(n_tm)])

    low, high, fix = edges(strain, taps)
    before = lax.ppermute(high, "tm", [(i, i + 1) for i in range(n_tm - 1)])
    after = lax.ppermute(low, "tm", [(i + 1, i) for i in range(n_tm - 1)])
    dec = decimate(strain, taps)

    asked = send_rows[0].reshape(n_tm, 2, n_sub, capacity).transpose(1, 0, 2, 3).reshape(1, 2, -1)
    asked = jnp.broadcast_to(asked, (n_tm,) + asked.shape[1:]).reshape(2 * n_tm, -1)
    asked = lax.all_to_all(asked, ("tm", "half"), 0, 0, tiled=True)
    asked = asked.reshape(n_tm, 2, n_tm * n_sub, capacity)
    asked_own = lax.dynamic_index_in_dim(asked, my_half, 1, keepdims=False)
    asked_mirrored = lax.dynamic_index_in_dim(asked, 1 - my_half, 1, keepdims=False)

    place = jnp.stack([my_tm, jnp.int32(n_tm)]).astype(jnp.int32)
    held = [whiten(place, dec, strain, before, after, fix, p, parts) for p in range(parts)]
    held = [list(half) for half in zip(*held)]
    mirrored = [[lax.ppermute(part, "half", swap) for part in half] for half in held]

    exchange = functools.partial(
        lax.all_to_all, axis_name=("tm", "sub"), split_axis=0, concat_axis=0, tiled=True
    )

    def by_segment(received):
        return received.reshape(n_tm, -1, received.shape[2])

    own = exchange(pick(asked_own, held))
    rows = jnp.concatenate([jnp.concatenate(half, axis=0) for half in held], axis=1)
    rows = rows.reshape(n_tm, -1, 4 * NH)
    receivers = [lax.dynamic_index_in_dim(rows, my_tm, 0, keepdims=False)]
    for a in range(1, n_tm):
        receivers.append(shifted(lax.dynamic_index_in_dim(rows, (my_tm + a) % n_tm, 0, keepdims=False), a))
    segment = (my_tm - jnp.arange(n_tm, dtype=jnp.int32)) % n_tm
    scalars = jnp.concatenate([pair_count, segment]).astype(jnp.int32)

    sender, column = pair_source[0] // capacity, pair_source[0] % capacity
    group, chan = sender // (2 * n_sub), sender % (2 * n_sub)
    half, sub = chan // n_sub, chan % n_sub
    slot = (sub * n_tm + group) * capacity + column
    slot += jnp.where(half == my_half, 0, n_sub * n_tm * capacity)
    ids = jnp.stack([slot, pair_receiver[0]], axis=1)

    outgoing = pick(asked_mirrored, [mirrored[0]])
    outgoing, own, mirrored[1][0], *receivers = lax.optimization_barrier((outgoing, own, mirrored[1][0], *receivers))
    others = exchange(outgoing)
    outgoing = pick(asked_mirrored, [mirrored[1]])
    outgoing, others = lax.optimization_barrier((outgoing, others))
    own = by_segment(own)
    partial = [correlate(scalars, ids, own, by_segment(others), receivers, 0, [])]
    others = exchange(outgoing)
    return correlate(scalars, ids, own, by_segment(others), receivers, 1, partial)[None]


def solution(mesh):
    n_tm, n_chan = mesh.devices.shape
    split = Mesh(mesh.devices.reshape(n_tm, 2, n_chan // 2), ("tm", "half", "sub"))
    device = ("tm", "half", "sub")
    return jax.shard_map(
        on_device,
        mesh=split,
        in_specs=(
            P("tm", ("half", "sub")),
            P(),
            P(device, None, None, None),
            P(device, None),
            P(device, None),
            P(device),
        ),
        out_specs=P(device, None, None),
        check_vma=False,
    )
```

```python
import functools
import math

import jax
import jax.numpy as jnp
import numpy as np
from jax import lax
from jax.experimental import pallas as pl
from jax.experimental.pallas import tpu as pltpu
from jax.sharding import Mesh
from jax.sharding import PartitionSpec as P

Q = 5
TAPS = 40
RIM = TAPS // 2
SEG = 1024
NF = 256
WF = 32
F0 = 40
TW = 32
WT = 64
LAGS = 256
BINS = NF + 2 * WF
TB = 128
FB = 64
RAW = 64
LEAD = 32
BAND = 384
NH = NF // 2
BF = jnp.bfloat16
F32 = jnp.float32
VMEM = 56 * 1024 * 1024
MOST = 52 * 1024 * 1024
PART = 24 * 1024 * 1024
TAIL = 59 * 1024 * 1024


def forward_table():
    phases = np.arange(F0 - WF, F0 + NF + WF)[:, None] * np.arange(SEG)[None, :] % SEG
    phases = phases * (2.0 * np.pi / SEG)
    return np.concatenate([np.cos(phases), -np.sin(phases)], axis=0).astype(BF)


def lag_table():
    phases = (F0 + np.arange(NF))[:, None] * (np.arange(LAGS) - LAGS // 2)[None, :] % SEG
    phases = phases * (2.0 * np.pi / SEG)
    return np.concatenate([np.cos(phases), -np.sin(phases)], axis=0).astype(BF)


def taper():
    bins = np.arange(NF)
    edge = np.minimum(bins, NF - 1 - bins)
    return np.where(edge < TW, 0.5 - 0.5 * np.cos(np.pi * (edge + 0.5) / TW), 1.0).astype(np.float32)


def ones_band(rows, columns, width):
    lag = np.arange(columns)[None, :] - np.arange(rows)[:, None]
    return ((lag >= 0) & (lag < width)).astype(BF)


def whole(shape):
    return pl.BlockSpec(shape, lambda *_: (0,) * len(shape))


def params(limit=VMEM):
    return pltpu.CompilerParams(vmem_limit_bytes=limit)


def fill_band(band_ref, taps_ref, work_ref, rows, shift):
    lanes = work_ref.shape[1]
    tap = lax.broadcasted_iota(jnp.int32, (8, 128), 1) - Q * lax.broadcasted_iota(jnp.int32, (8, 128), 0)
    pattern = jnp.zeros((8, 128), F32)
    for k in range(TAPS):
        pattern = jnp.where(tap == k, taps_ref[k], pattern)
    pattern = jnp.concatenate([pattern, jnp.zeros((8, lanes - 128), F32)], axis=1)
    for m in range(0, rows, 8):
        work_ref[m : m + 8] = pltpu.roll(pattern, (Q * m + shift) % lanes, 1)
    values = work_ref[:rows, : band_ref.shape[1]]
    upper = values.astype(BF)
    band_ref[:rows] = upper
    band_ref[rows:] = (values - upper.astype(F32)).astype(BF)


def filtered(band, x):
    both = jnp.dot(band, x, preferred_element_type=F32)
    rows = both.shape[0] // 2
    return (both[:rows] + both[rows:]).astype(BF)


EDGE = 352


def edge_kernel(taps_ref, x_ref, low_ref, high_ref, fix_ref, low, high, low_band, high_band, work, arrived):
    fetch_low = pltpu.make_async_copy(x_ref.at[pl.ds(0, EDGE)], low, arrived.at[0])
    fetch_high = pltpu.make_async_copy(x_ref.at[pl.ds(x_ref.shape[0] - EDGE, EDGE)], high, arrived.at[1])
    fetch_low.start()
    fetch_high.start()
    fill_band(low_band, taps_ref, work, WT, -RIM)
    fill_band(high_band, taps_ref, work, WT, EDGE - Q * WT - RIM)
    fill_band(fix_ref, taps_ref, work, 16, RAW - Q * 8 - RIM)
    fetch_low.wait()
    low_ref[:RAW] = low[:RAW]
    low_ref[RAW:] = filtered(low_band[...], low[...])
    fetch_high.wait()
    high_ref[:RAW] = high[EDGE - RAW :]
    high_ref[RAW:] = filtered(high_band[...], high[...])


def edges(x, taps):
    width = x.shape[1]
    in_vmem = pl.BlockSpec(memory_space=pltpu.VMEM)
    return pl.pallas_call(
        edge_kernel,
        in_specs=[pl.BlockSpec(memory_space=pltpu.SMEM), pl.BlockSpec(memory_space=pl.ANY)],
        out_specs=[in_vmem] * 3,
        out_shape=[
            jax.ShapeDtypeStruct((RAW + WT, width), BF),
            jax.ShapeDtypeStruct((RAW + WT, width), BF),
            jax.ShapeDtypeStruct((32, 2 * RAW), BF),
        ],
        scratch_shapes=[
            pltpu.VMEM((EDGE, width), BF),
            pltpu.VMEM((EDGE, width), BF),
            pltpu.VMEM((2 * WT, EDGE), BF),
            pltpu.VMEM((2 * WT, EDGE), BF),
            pltpu.VMEM((WT, 512), F32),
            pltpu.SemaphoreType.DMA((2,)),
        ],
        compiler_params=params(MOST),
    )(taps, x)


def decimate_kernel(taps_ref, x_ref, out_ref, x, main, first, work, arrived):
    length = out_ref.shape[0]
    fetches = arrived.shape[0]
    each = Q * length // fetches

    def fetch(k):
        rows = pl.ds(each * k, each)
        return pltpu.make_async_copy(x_ref.at[rows], x.at[rows], arrived.at[k])

    for k in range(fetches):
        fetch(k).start()
    fill_band(main, taps_ref, work, FB, LEAD - RIM)
    fill_band(first, taps_ref, work, FB, -RIM)
    here = 0
    for b in range(length // FB):
        start = max(Q * FB * b - LEAD, 0)
        stop = min(Q * FB * b - LEAD + BAND, Q * length)
        while each * here < stop:
            fetch(here).wait()
            here += 1
        band = first[...] if b == 0 else main[:, : stop - start]
        out_ref[FB * b : FB * (b + 1)] = filtered(band, x[start:stop])


def decimate(x, taps):
    rows, width = x.shape
    return pl.pallas_call(
        decimate_kernel,
        in_specs=[pl.BlockSpec(memory_space=pltpu.SMEM), pl.BlockSpec(memory_space=pl.ANY)],
        out_specs=pl.BlockSpec(memory_space=pltpu.VMEM),
        out_shape=jax.ShapeDtypeStruct((rows // Q, width), BF),
        scratch_shapes=[
            pltpu.VMEM((rows, width), BF),
            pltpu.VMEM((2 * FB, BAND), BF),
            pltpu.VMEM((2 * FB, BAND - LEAD), BF),
            pltpu.VMEM((FB, 512), F32),
            pltpu.SemaphoreType.DMA((8,)),
        ],
        compiler_params=params(MOST),
    )(taps, x)


def inverse(values):
    guess = pl.reciprocal(values, approx=True)
    return guess * (2.0 - values * guess)


def whiten_kernel(
    place_ref, dec_ref, first_ref, last_ref, before_ref, after_ref, fix_ref, ones_ref, table_ref, smooth_ref,
    taper_ref, low_ref, high_ref, size, flat
):
    length = dec_ref.shape[0]
    blocks = length // TB
    place, count = place_ref[0], place_ref[1]
    low = filtered(fix_ref[...], jnp.concatenate([before_ref[:RAW], first_ref[...]])).astype(F32)
    high = filtered(fix_ref[...], jnp.concatenate([last_ref[...], after_ref[:RAW]])).astype(F32)
    before = jnp.concatenate([before_ref[RAW:].astype(F32)[:-8], low[:8]])
    after = jnp.concatenate([high[8:], after_ref[RAW:].astype(F32)[8:]])
    size[:WT] = jnp.abs(jnp.where(place > 0, before, 0.0)).astype(BF)
    size[WT + length :] = jnp.abs(jnp.where(place < count - 1, after, 0.0)).astype(BF)
    flat[...] = dec_ref[...]
    flat[:TB] = jnp.concatenate([low[8:], dec_ref[:TB].astype(F32)[8:]]).astype(BF)
    flat[length - TB :] = jnp.concatenate([dec_ref[length - TB :].astype(F32)[:-8], high[:8]]).astype(BF)
    size[WT : WT + length] = jnp.abs(flat[...])
    for b in range(blocks):
        mean = jnp.dot(ones_ref[...], size[TB * b : TB * b + TB + 2 * WT], preferred_element_type=F32)
        if b == 0 or b == blocks - 1:
            sample = place * length + TB * b + lax.broadcasted_iota(jnp.int32, (TB, 1), 0)
            total = jnp.minimum(sample + WT, count * length - 1) - jnp.maximum(sample - WT, 0) + 1
            mean = mean / total.astype(F32)
        else:
            mean = mean * (1.0 / (2 * WT + 1))
        rows = slice(TB * b, TB * (b + 1))
        flat[rows] = (flat[rows].astype(F32) * inverse(mean + 1e-05)).astype(BF)
    spectrum = jnp.dot(table_ref[...], flat[...], preferred_element_type=F32)
    real, imag = spectrum[:BINS], spectrum[BINS:]
    magnitude = jnp.sqrt(real * real + imag * imag)
    smooth = jnp.dot(smooth_ref[...], magnitude.astype(BF), preferred_element_type=F32)
    factor = taper_ref[...] * inverse(smooth * (1.0 / (2 * WF + 1)) + 1e-05)
    real, imag = real[WF : WF + NF] * factor, imag[WF : WF + NF] * factor
    low_ref[:, :NH] = real[:NH].T.astype(BF)
    low_ref[:, NH:] = imag[:NH].T.astype(BF)
    high_ref[:, :NH] = real[NH:].T.astype(BF)
    high_ref[:, NH:] = imag[NH:].T.astype(BF)


def whiten(place, dec, low, high, before, after, fix, start, held):
    length, width = dec.shape
    chunk = 256 if width % 256 == 0 else 128
    first = start // chunk
    tables = (
        ones_band(TB, TB + 2 * WT, 2 * WT + 1),
        forward_table(),
        ones_band(NF, BINS, 2 * WF + 1),
        taper()[:, None],
    )
    column = lambda c: (0, first + c)
    return pl.pallas_call(
        whiten_kernel,
        grid=(held // chunk,),
        in_specs=[
            pl.BlockSpec(memory_space=pltpu.SMEM),
            pl.BlockSpec((length, chunk), column),
            pl.BlockSpec((RAW, chunk), column),
            pl.BlockSpec((RAW, chunk), column),
            pl.BlockSpec((RAW + WT, chunk), column),
            pl.BlockSpec((RAW + WT, chunk), column),
            whole(fix.shape),
        ]
        + [whole(table.shape) for table in tables],
        out_specs=[pl.BlockSpec((chunk, 2 * NH), lambda c: (c, 0))] * 2,
        out_shape=[jax.ShapeDtypeStruct((held, 2 * NH), BF)] * 2,
        scratch_shapes=[pltpu.VMEM((length + 2 * WT, chunk), BF), pltpu.VMEM((length, chunk), BF)],
        compiler_params=params(PART),
    )(place, dec, low, high, before, after, fix, *tables)


def one_hot(ids, columns):
    wide = -(-columns // 128)
    lane = lax.broadcasted_iota(jnp.int32, (128, 128 * wide), 1)
    parts = []
    for r in range(ids.shape[0]):
        column = jnp.broadcast_to(ids[r : r + 1].astype(F32), (128, 128)).T.astype(jnp.int32)
        hits = jnp.concatenate([column] * wide, axis=1) == lane
        parts.append(jnp.where(hits, 1.0, 0.0).astype(BF)[:, :columns])
    return jnp.concatenate(parts, axis=0)


def pick_kernel(ids_ref, *refs):
    *halves, out_ref = refs
    owners, rows, _ = out_ref.shape
    hot = one_hot(ids_ref[0], halves[0].shape[0])
    for h, half in enumerate(halves):
        picked = jnp.dot(hot, half[...], preferred_element_type=F32).astype(BF)
        out_ref[:, :, 2 * NH * h : 2 * NH * (h + 1)] = picked.reshape(owners, rows, 2 * NH)


def pick(ids, halves, capacity):
    groups = ids.shape[0]
    owners = ids.size // groups // capacity
    width = 2 * NH * len(halves)
    join = 1
    while join * capacity % 16 != 0:
        join *= 2
    steps = groups // join
    held = halves[0].shape[0] // steps
    rows = owners * join * capacity
    if join > 1:
        ids = ids.reshape(steps, join, owners, capacity).transpose(0, 2, 1, 3)
        ids = ids + (jnp.arange(join, dtype=jnp.int32) * (held // join))[None, None, :, None]
    return pl.pallas_call(
        pick_kernel,
        grid=(steps,),
        in_specs=[pl.BlockSpec((1, rows // 128, 128), lambda g: (g, 0, 0))]
        + [pl.BlockSpec((held, 2 * NH), lambda g: (g, 0)) for _ in halves],
        out_specs=pl.BlockSpec((owners, join * capacity, width), lambda g: (0, g, 0)),
        out_shape=jax.ShapeDtypeStruct((owners, groups * capacity, width), BF),
        compiler_params=params(PART),
    )(ids.reshape(steps, rows // 128, 128), *halves)


def pair_block(pairs, segments):
    return min(pairs, 512 if segments <= 4 else 128)


def ids_spec(block):
    return pl.BlockSpec((1, block // 128, 128), lambda p: (p, 0, 0))


def once(shape):
    return pl.BlockSpec(shape, lambda p: (0,) * len(shape), pipeline_mode=pl.Buffered(1))


def receive_kernel(ids_ref, *refs):
    receivers, (low_ref, high_ref) = refs[:-2], refs[-2:]
    hot = one_hot(ids_ref[0], receivers[0].shape[0])
    for k, rows in enumerate(receivers):
        low_ref[k] = jnp.dot(hot, rows[:, : 2 * NH], preferred_element_type=F32).astype(BF)
        high_ref[k] = jnp.dot(hot, rows[:, 2 * NH :], preferred_element_type=F32).astype(BF)


def receive(ids, receivers):
    segments, pairs = len(receivers), ids.size
    block = pair_block(pairs, segments)
    rows = pl.BlockSpec((segments, block, 2 * NH), lambda p: (0, p, 0))
    return pl.pallas_call(
        receive_kernel,
        grid=(pairs // block,),
        in_specs=[ids_spec(block)] + [once(r.shape) for r in receivers],
        out_specs=[rows, rows],
        out_shape=[jax.ShapeDtypeStruct((segments, pairs, 2 * NH), BF)] * 2,
        compiler_params=params(),
    )(ids.reshape(-1, block // 128, 128), *receivers)


def cross(hot, segment_ref, rows_ref, lanes, receiver_ref):
    real = imag = None
    for k in range(receiver_ref.shape[0]):
        a = jnp.dot(hot, rows_ref[segment_ref[k], :, lanes], preferred_element_type=F32)
        b = receiver_ref[k].astype(F32)
        a_re, a_im, b_re, b_im = a[:, :NH], a[:, NH:], b[:, :NH], b[:, NH:]
        re = a_re * b_re + a_im * b_im
        im = a_im * b_re - a_re * b_im
        real = re if k == 0 else real + re
        imag = im if k == 0 else imag + im
    return jnp.concatenate([real, imag], axis=1).astype(BF)


def own_kernel(segment_ref, ids_ref, own_ref, low_ref, high_ref, low_out, high_out):
    hot = one_hot(ids_ref[0], own_ref.shape[1])
    low_out[...] = cross(hot, segment_ref, own_ref, slice(0, 2 * NH), low_ref)
    high_out[...] = cross(hot, segment_ref, own_ref, slice(2 * NH, 4 * NH), high_ref)


def cross_own(segment, ids, own, low, high):
    segments, pairs, _ = low.shape
    block = pair_block(pairs, segments)
    rows = pl.BlockSpec((segments, block, 2 * NH), lambda p: (0, p, 0))
    out = pl.BlockSpec((block, 2 * NH), lambda p: (p, 0))
    return pl.pallas_call(
        own_kernel,
        grid=(pairs // block,),
        in_specs=[pl.BlockSpec(memory_space=pltpu.SMEM), ids_spec(block), once(own.shape), rows, rows],
        out_specs=[out, out],
        out_shape=[jax.ShapeDtypeStruct((pairs, 2 * NH), BF)] * 2,
        compiler_params=params(),
    )(segment, ids.reshape(-1, block // 128, 128), own, low, high)


def mirrored_kernel(segment_ref, ids_ref, rows_ref, receiver_ref, own_ref, out_ref):
    held = rows_ref.shape[1]
    hot = one_hot(ids_ref[0] - held, held)
    out_ref[...] = own_ref[...] + cross(hot, segment_ref, rows_ref, slice(None), receiver_ref)


def cross_mirrored(segment, ids, rows, receiver, own):
    segments, pairs, _ = receiver.shape
    block = pair_block(pairs, segments)
    out = pl.BlockSpec((block, 2 * NH), lambda p: (p, 0))
    return pl.pallas_call(
        mirrored_kernel,
        grid=(pairs // block,),
        in_specs=[
            pl.BlockSpec(memory_space=pltpu.SMEM),
            ids_spec(block),
            once(rows.shape),
            pl.BlockSpec((segments, block, 2 * NH), lambda p: (0, p, 0)),
            out,
        ],
        out_specs=out,
        out_shape=jax.ShapeDtypeStruct((pairs, 2 * NH), BF),
        compiler_params=params(TAIL),
    )(segment, ids.reshape(-1, block // 128, 128), rows, receiver, own)


def lags_kernel(segment_ref, count_ref, ids_ref, rows_ref, receiver_ref, own_ref, low_ref, table_ref, out_ref):
    pairs = out_ref.shape[0]
    held = rows_ref.shape[1]
    hot = one_hot(ids_ref[0] - held, held)
    high = own_ref[...] + cross(hot, segment_ref, rows_ref, slice(None), receiver_ref)
    values = jnp.dot(low_ref[...], table_ref[: 2 * NH], preferred_element_type=F32)
    values += jnp.dot(high, table_ref[2 * NH :], preferred_element_type=F32)
    place = pl.program_id(0) * pairs + lax.broadcasted_iota(jnp.int32, values.shape, 0)
    scale = 1.0 / math.sqrt(receiver_ref.shape[0] * NF)
    out_ref[...] = jnp.where(place < count_ref[0], values * scale, 0.0)


def lags(segment, count, ids, rows, receiver, own, low):
    segments, pairs, _ = receiver.shape
    block = pair_block(pairs, segments)
    table = lag_table().reshape(2, 2, NH, LAGS).transpose(1, 0, 2, 3).reshape(4 * NH, LAGS)
    bins = pl.BlockSpec((block, 2 * NH), lambda p: (p, 0))
    return pl.pallas_call(
        lags_kernel,
        grid=(pairs // block,),
        in_specs=[
            pl.BlockSpec(memory_space=pltpu.SMEM),
            pl.BlockSpec(memory_space=pltpu.SMEM),
            ids_spec(block),
            once(rows.shape),
            pl.BlockSpec((segments, block, 2 * NH), lambda p: (0, p, 0)),
            bins,
            bins,
            whole(table.shape),
        ],
        out_specs=pl.BlockSpec((block, LAGS), lambda p: (p, 0)),
        out_shape=jax.ShapeDtypeStruct((pairs, LAGS), F32),
        compiler_params=params(TAIL),
    )(segment, count, ids.reshape(-1, block // 128, 128), rows, receiver, own, low, table)


def on_device(strain, taps, send_rows, pair_source, pair_receiver, pair_count):
    n_tm, n_sub = lax.axis_size("tm"), lax.axis_size("sub")
    my_tm, my_half = lax.axis_index("tm"), lax.axis_index("half")
    capacity = send_rows.shape[3]
    width = strain.shape[1]
    split = [512, width - 512] if width % 256 == 0 and width > 512 else [width]
    order = (my_tm - jnp.arange(n_tm, dtype=jnp.int32)) % n_tm

    def shifted(array, by):
        return lax.ppermute(array, "tm", [(i, (i + by) % n_tm) for i in range(n_tm)])

    def across(array, by=0):
        pairs = [(2 * i + h, (i + by) % n_tm * 2 + 1 - h) for i in range(n_tm) for h in range(2)]
        return lax.ppermute(array, ("tm", "half"), pairs)

    def exchange(array):
        return lax.all_to_all(array, ("tm", "sub"), 0, 0, tiled=True)

    def by_segment(array):
        return array.reshape(n_tm, -1, array.shape[2])

    asked = send_rows[0].reshape(n_tm, 2, -1).transpose(1, 0, 2).reshape(1, 2, -1, 128)
    asked = jnp.broadcast_to(asked, (n_tm,) + asked.shape[1:]).reshape((2 * n_tm,) + asked.shape[2:])
    first, last, fix = edges(strain, taps)
    before = lax.ppermute(last, "tm", [(i, i + 1) for i in range(n_tm - 1)])
    after = lax.ppermute(first, "tm", [(i + 1, i) for i in range(n_tm - 1)])
    asked, first, last = lax.optimization_barrier((asked, first, last))
    asked = lax.all_to_all(asked, ("tm", "half"), 0, 0, tiled=True)
    asked = asked.reshape(n_tm, 2, -1, 128)

    dec = decimate(strain, taps)
    place = jnp.stack([my_tm, jnp.int32(n_tm)]).astype(jnp.int32)
    starts = [sum(split[:p]) for p in range(len(split))]
    parts = [whiten(place, dec, first, last, before, after, fix, *part) for part in zip(starts, split)]
    low, high = [list(half) for half in zip(*parts)]

    low_across = [across(part) for part in low]
    high_across = [across(part) for part in high[::-1]][::-1]

    low, high = jnp.concatenate(low, axis=0), jnp.concatenate(high, axis=0)
    asked_own = lax.dynamic_index_in_dim(asked, my_half, 1, keepdims=False)
    outgoing = pick(asked_own, [low, high], capacity)
    outgoing, low_across[0] = lax.optimization_barrier((outgoing, low_across[0]))
    own = exchange(outgoing)
    receivers = []
    for a in range(n_tm):
        at = (my_tm + a) % n_tm * (width // n_tm)
        rows = [lax.dynamic_slice_in_dim(half, at, width // n_tm, 0) for half in (low, high)]
        rows = jnp.concatenate(rows, axis=1)
        receivers.append(shifted(rows, a) if a else rows)

    asked_other = lax.dynamic_index_in_dim(asked, 1 - my_half, 1, keepdims=False)

    sender, column = pair_source[0] // capacity, pair_source[0] % capacity
    group, chan = sender // (2 * n_sub), sender % (2 * n_sub)
    slot = (chan % n_sub * n_tm + group) * capacity + column
    slot += jnp.where(chan // n_sub == my_half, 0, n_sub * n_tm * capacity)

    outgoing = pick(asked_other, [jnp.concatenate(low_across, axis=0)], capacity)
    outgoing, own, high_across[-1], *receivers = lax.optimization_barrier(
        (outgoing, own, high_across[-1], *receivers)
    )
    others = exchange(outgoing)
    receiver = receive(pair_receiver[0], receivers)
    bins = cross_own(order, slot, by_segment(own), *receiver)
    *bins, high_across[0] = lax.optimization_barrier((*bins, high_across[0]))
    outgoing = pick(asked_other, [jnp.concatenate(high_across, axis=0)], capacity)
    outgoing, others = lax.optimization_barrier((outgoing, others))
    bins[0] = cross_mirrored(order, slot, by_segment(others), receiver[0], bins[0])
    others = exchange(outgoing)
    return lags(order, pair_count, slot, by_segment(others), receiver[1], bins[1], bins[0])[None]


def solution(mesh):
    n_tm, n_chan = mesh.devices.shape
    split = Mesh(mesh.devices.reshape(n_tm, 2, n_chan // 2), ("tm", "half", "sub"))
    device = ("tm", "half", "sub")
    return jax.shard_map(
        on_device,
        mesh=split,
        in_specs=(
            P("tm", ("half", "sub")),
            P(),
            P(device, None, None, None),
            P(device, None),
            P(device, None),
            P(device),
        ),
        out_specs=P(device, None, None),
        check_vma=False,
    )
```

```python
import functools
import math

import jax
import jax.numpy as jnp
import numpy as np
from jax import lax
from jax.experimental import pallas as pl
from jax.experimental.pallas import tpu as pltpu
from jax.sharding import Mesh
from jax.sharding import PartitionSpec as P

Q = 5
TAPS = 40
RIM = TAPS // 2
SEG = 1024
NF = 256
WF = 32
F0 = 40
TW = 32
WT = 64
LAGS = 256
BINS = NF + 2 * WF
TB = 128
FB = 64
RAW = 64
LEAD = 32
BAND = 384
NH = NF // 2
BF = jnp.bfloat16
F32 = jnp.float32
VMEM = 56 * 1024 * 1024
MOST = 52 * 1024 * 1024
PART = 24 * 1024 * 1024
TAIL = 59 * 1024 * 1024


def forward_table():
    phases = np.arange(F0 - WF, F0 + NF + WF)[:, None] * np.arange(SEG)[None, :] % SEG
    phases = phases * (2.0 * np.pi / SEG)
    return np.concatenate([np.cos(phases), -np.sin(phases)], axis=0).astype(BF)


def lag_table():
    phases = (F0 + np.arange(NF))[:, None] * (np.arange(LAGS) - LAGS // 2)[None, :] % SEG
    phases = phases * (2.0 * np.pi / SEG)
    return np.concatenate([np.cos(phases), -np.sin(phases)], axis=0).astype(BF)


def taper():
    bins = np.arange(NF)
    edge = np.minimum(bins, NF - 1 - bins)
    return np.where(edge < TW, 0.5 - 0.5 * np.cos(np.pi * (edge + 0.5) / TW), 1.0).astype(np.float32)


def ones_band(rows, columns, width):
    lag = np.arange(columns)[None, :] - np.arange(rows)[:, None]
    return ((lag >= 0) & (lag < width)).astype(BF)


COST = (69000000000, 69000000000)


def whole(shape):
    return pl.BlockSpec(shape, lambda *_: (0,) * len(shape))


def params(limit=VMEM):
    return pltpu.CompilerParams(vmem_limit_bytes=limit)


def fill_band(band_ref, taps_ref, work_ref, rows, shift):
    lanes = work_ref.shape[1]
    tap = lax.broadcasted_iota(jnp.int32, (8, 128), 1) - Q * lax.broadcasted_iota(jnp.int32, (8, 128), 0)
    pattern = jnp.zeros((8, 128), F32)
    for k in range(TAPS):
        pattern = jnp.where(tap == k, taps_ref[k], pattern)
    pattern = jnp.concatenate([pattern, jnp.zeros((8, lanes - 128), F32)], axis=1)
    for m in range(0, rows, 8):
        work_ref[m : m + 8] = pltpu.roll(pattern, (Q * m + shift) % lanes, 1)
    values = work_ref[:rows, : band_ref.shape[1]]
    upper = values.astype(BF)
    band_ref[:rows] = upper
    band_ref[rows:] = (values - upper.astype(F32)).astype(BF)


def filtered(band, x):
    both = jnp.dot(band, x, preferred_element_type=F32)
    rows = both.shape[0] // 2
    return (both[:rows] + both[rows:]).astype(BF)


EDGE = 352


def edge_kernel(taps_ref, x_ref, low_ref, high_ref, fix_ref, low, high, low_band, high_band, work, arrived):
    fetch_low = pltpu.make_async_copy(x_ref.at[pl.ds(0, EDGE)], low, arrived.at[0])
    fetch_high = pltpu.make_async_copy(x_ref.at[pl.ds(x_ref.shape[0] - EDGE, EDGE)], high, arrived.at[1])
    fetch_low.start()
    fetch_high.start()
    fill_band(low_band, taps_ref, work, WT, -RIM)
    fill_band(high_band, taps_ref, work, WT, EDGE - Q * WT - RIM)
    fill_band(fix_ref, taps_ref, work, 16, RAW - Q * 8 - RIM)
    fetch_low.wait()
    low_ref[:RAW] = low[:RAW]
    low_ref[RAW:] = filtered(low_band[...], low[...])
    fetch_high.wait()
    high_ref[:RAW] = high[EDGE - RAW :]
    high_ref[RAW:] = filtered(high_band[...], high[...])


def edges(x, taps):
    width = x.shape[1]
    in_vmem = pl.BlockSpec(memory_space=pltpu.VMEM)
    return pl.pallas_call(
        edge_kernel,
        in_specs=[pl.BlockSpec(memory_space=pltpu.SMEM), pl.BlockSpec(memory_space=pl.ANY)],
        out_specs=[in_vmem] * 3,
        out_shape=[
            jax.ShapeDtypeStruct((RAW + WT, width), BF),
            jax.ShapeDtypeStruct((RAW + WT, width), BF),
            jax.ShapeDtypeStruct((32, 2 * RAW), BF),
        ],
        scratch_shapes=[
            pltpu.VMEM((EDGE, width), BF),
            pltpu.VMEM((EDGE, width), BF),
            pltpu.VMEM((2 * WT, EDGE), BF),
            pltpu.VMEM((2 * WT, EDGE), BF),
            pltpu.VMEM((WT, 512), F32),
            pltpu.SemaphoreType.DMA((2,)),
        ],
        compiler_params=params(MOST),
    )(taps, x)


def decimate_kernel(taps_ref, x_ref, out_ref, x, main, first, work, arrived):
    length = out_ref.shape[0]
    fetches = arrived.shape[0]
    each = Q * length // fetches

    def fetch(k):
        rows = pl.ds(each * k, each)
        return pltpu.make_async_copy(x_ref.at[rows], x.at[rows], arrived.at[k])

    for k in range(fetches):
        fetch(k).start()
    fill_band(main, taps_ref, work, FB, LEAD - RIM)
    fill_band(first, taps_ref, work, FB, -RIM)
    here = 0
    for b in range(length // FB):
        start = max(Q * FB * b - LEAD, 0)
        stop = min(Q * FB * b - LEAD + BAND, Q * length)
        while each * here < stop:
            fetch(here).wait()
            here += 1
        band = first[...] if b == 0 else main[:, : stop - start]
        out_ref[FB * b : FB * (b + 1)] = filtered(band, x[start:stop])


def decimate(x, taps):
    rows, width = x.shape
    return pl.pallas_call(
        decimate_kernel,
        in_specs=[pl.BlockSpec(memory_space=pltpu.SMEM), pl.BlockSpec(memory_space=pl.ANY)],
        out_specs=pl.BlockSpec(memory_space=pltpu.VMEM),
        out_shape=jax.ShapeDtypeStruct((rows // Q, width), BF),
        scratch_shapes=[
            pltpu.VMEM((rows, width), BF),
            pltpu.VMEM((2 * FB, BAND), BF),
            pltpu.VMEM((2 * FB, BAND - LEAD), BF),
            pltpu.VMEM((FB, 512), F32),
            pltpu.SemaphoreType.DMA((8,)),
        ],
        compiler_params=params(MOST),
    )(taps, x)


def inverse(values):
    guess = pl.reciprocal(values, approx=True)
    return guess * (2.0 - values * guess)


def whiten_kernel(
    place_ref, dec_ref, first_ref, last_ref, before_ref, after_ref, fix_ref, ones_ref, table_ref, smooth_ref,
    taper_ref, out_ref, size, flat
):
    length = dec_ref.shape[0]
    blocks = length // TB
    place, count = place_ref[0], place_ref[1]
    low = filtered(fix_ref[...], jnp.concatenate([before_ref[:RAW], first_ref[...]])).astype(F32)
    high = filtered(fix_ref[...], jnp.concatenate([last_ref[...], after_ref[:RAW]])).astype(F32)
    before = jnp.concatenate([before_ref[RAW:].astype(F32)[:-8], low[:8]])
    after = jnp.concatenate([high[8:], after_ref[RAW:].astype(F32)[8:]])
    size[:WT] = jnp.abs(jnp.where(place > 0, before, 0.0)).astype(BF)
    size[WT + length :] = jnp.abs(jnp.where(place < count - 1, after, 0.0)).astype(BF)
    flat[...] = dec_ref[...]
    flat[:TB] = jnp.concatenate([low[8:], dec_ref[:TB].astype(F32)[8:]]).astype(BF)
    flat[length - TB :] = jnp.concatenate([dec_ref[length - TB :].astype(F32)[:-8], high[:8]]).astype(BF)
    size[WT : WT + length] = jnp.abs(flat[...])
    for b in range(blocks):
        mean = jnp.dot(ones_ref[...], size[TB * b : TB * b + TB + 2 * WT], preferred_element_type=F32)
        if b == 0 or b == blocks - 1:
            sample = place * length + TB * b + lax.broadcasted_iota(jnp.int32, (TB, 1), 0)
            total = jnp.minimum(sample + WT, count * length - 1) - jnp.maximum(sample - WT, 0) + 1
            mean = mean / total.astype(F32)
        else:
            mean = mean * (1.0 / (2 * WT + 1))
        rows = slice(TB * b, TB * (b + 1))
        flat[rows] = (flat[rows].astype(F32) * inverse(mean + 1e-05)).astype(BF)
    spectrum = jnp.dot(table_ref[...], flat[...], preferred_element_type=F32)
    real, imag = spectrum[:BINS], spectrum[BINS:]
    magnitude = jnp.sqrt(real * real + imag * imag)
    smooth = jnp.dot(smooth_ref[...], magnitude.astype(BF), preferred_element_type=F32)
    factor = taper_ref[...] * inverse(smooth * (1.0 / (2 * WF + 1)) + 1e-05)
    real, imag = real[WF : WF + NF] * factor, imag[WF : WF + NF] * factor
    out_ref[:, :NH] = real[:NH].T.astype(BF)
    out_ref[:, NH : 2 * NH] = imag[:NH].T.astype(BF)
    out_ref[:, 2 * NH : 3 * NH] = real[NH:].T.astype(BF)
    out_ref[:, 3 * NH :] = imag[NH:].T.astype(BF)


def whiten(place, dec, low, high, before, after, fix, start, held):
    length, width = dec.shape
    chunk = held
    first = start // chunk
    tables = (
        ones_band(TB, TB + 2 * WT, 2 * WT + 1),
        forward_table(),
        ones_band(NF, BINS, 2 * WF + 1),
        taper()[:, None],
    )
    column = lambda c: (0, first + c)
    return pl.pallas_call(
        whiten_kernel,
        grid=(held // chunk,),
        in_specs=[
            pl.BlockSpec(memory_space=pltpu.SMEM),
            pl.BlockSpec((length, chunk), column),
            pl.BlockSpec((RAW, chunk), column),
            pl.BlockSpec((RAW, chunk), column),
            pl.BlockSpec((RAW + WT, chunk), column),
            pl.BlockSpec((RAW + WT, chunk), column),
            whole(fix.shape),
        ]
        + [whole(table.shape) for table in tables],
        out_specs=pl.BlockSpec((chunk, 4 * NH), lambda c: (c, 0)),
        out_shape=jax.ShapeDtypeStruct((held, 4 * NH), BF),
        scratch_shapes=[pltpu.VMEM((length + 2 * WT, chunk), BF), pltpu.VMEM((length, chunk), BF)],
        compiler_params=params(VMEM),
    )(place, dec, low, high, before, after, fix, *tables)


def one_hot(ids, columns):
    wide = -(-columns // 128)
    lane = lax.broadcasted_iota(jnp.int32, (128, 128 * wide), 1)
    parts = []
    for r in range(ids.shape[0]):
        column = jnp.broadcast_to(ids[r : r + 1].astype(F32), (128, 128)).T.astype(jnp.int32)
        hits = jnp.concatenate([column] * wide, axis=1) == lane
        parts.append(jnp.where(hits, 1.0, 0.0).astype(BF)[:, :columns])
    return jnp.concatenate(parts, axis=0)


def pick_kernel(ids_ref, rows_ref, *refs):
    out_ref = refs[-1]
    owners, rows, width = out_ref.shape
    hot = one_hot(ids_ref[0], rows_ref.shape[0])
    for lane in range(0, width, 2 * NH):
        picked = jnp.dot(hot, rows_ref[:, lane : lane + 2 * NH], preferred_element_type=F32).astype(BF)
        out_ref[:, :, lane : lane + 2 * NH] = picked.reshape(owners, rows, 2 * NH)


def pick(ids, spectra, capacity, part, parts, filled, cost=None):
    groups = ids.shape[0] // parts
    owners = ids.size // ids.shape[0] // capacity
    width = spectra.shape[1]
    join = 1
    while join * capacity % 16 != 0:
        join *= 2
    steps = groups // join
    held = spectra.shape[0] // steps
    rows = owners * join * capacity
    ids = ids[part * groups : (part + 1) * groups]
    if join > 1:
        ids = ids.reshape(steps, join, owners, capacity).transpose(0, 2, 1, 3)
        ids = ids + (jnp.arange(join, dtype=jnp.int32) * (held // join))[None, None, :, None]
    return pl.pallas_call(
        pick_kernel,
        grid=(steps,),
        in_specs=[
            pl.BlockSpec((1, rows // 128, 128), lambda g: (g, 0, 0)),
            pl.BlockSpec((held, width), lambda g: (g, 0)),
        ]
        + [pl.BlockSpec(memory_space=pl.ANY) for _ in filled],
        out_specs=pl.BlockSpec((owners, join * capacity, width), lambda g: (0, part * steps + g, 0)),
        out_shape=jax.ShapeDtypeStruct((owners, parts * groups * capacity, width), BF),
        input_output_aliases={2: 0} if filled else {},
        compiler_params=params(PART),
        cost_estimate=cost,
    )(ids.reshape(steps, rows // 128, 128), spectra, *filled)


def pair_block(pairs, segments):
    return min(pairs, 512 if segments <= 4 else 128)


def ids_spec(block):
    return pl.BlockSpec((1, block // 128, 128), lambda p: (p, 0, 0))


def once(shape):
    return pl.BlockSpec(shape, lambda p: (0,) * len(shape), pipeline_mode=pl.Buffered(1))


def receive_kernel(ids_ref, *refs):
    receivers, (low_ref, high_ref) = refs[:-2], refs[-2:]
    hot = one_hot(ids_ref[0], receivers[0].shape[0])
    for k, rows in enumerate(receivers):
        low_ref[k] = jnp.dot(hot, rows[:, : 2 * NH], preferred_element_type=F32).astype(BF)
        high_ref[k] = jnp.dot(hot, rows[:, 2 * NH :], preferred_element_type=F32).astype(BF)


def receive(ids, receivers):
    segments, pairs = len(receivers), ids.size
    block = pair_block(pairs, segments)
    rows = pl.BlockSpec((segments, block, 2 * NH), lambda p: (0, p, 0))
    return pl.pallas_call(
        receive_kernel,
        grid=(pairs // block,),
        in_specs=[ids_spec(block)] + [once(r.shape) for r in receivers],
        out_specs=[rows, rows],
        out_shape=[jax.ShapeDtypeStruct((segments, pairs, 2 * NH), BF)] * 2,
        compiler_params=params(),
    )(ids.reshape(-1, block // 128, 128), *receivers)


def cross(hot, segment_ref, rows_ref, lanes, receiver_ref):
    real = imag = None
    for k in range(receiver_ref.shape[0]):
        a = jnp.dot(hot, rows_ref[segment_ref[k], :, lanes], preferred_element_type=F32)
        b = receiver_ref[k].astype(F32)
        a_re, a_im, b_re, b_im = a[:, :NH], a[:, NH:], b[:, :NH], b[:, NH:]
        re = a_re * b_re + a_im * b_im
        im = a_im * b_re - a_re * b_im
        real = re if k == 0 else real + re
        imag = im if k == 0 else imag + im
    return jnp.concatenate([real, imag], axis=1).astype(BF)


def own_kernel(segment_ref, ids_ref, own_ref, low_ref, high_ref, low_out, high_out):
    hot = one_hot(ids_ref[0], own_ref.shape[1])
    low_out[...] = cross(hot, segment_ref, own_ref, slice(0, 2 * NH), low_ref)
    high_out[...] = cross(hot, segment_ref, own_ref, slice(2 * NH, 4 * NH), high_ref)


def cross_own(segment, ids, own, low, high):
    segments, pairs, _ = low.shape
    block = pair_block(pairs, segments)
    rows = pl.BlockSpec((segments, block, 2 * NH), lambda p: (0, p, 0))
    out = pl.BlockSpec((block, 2 * NH), lambda p: (p, 0))
    return pl.pallas_call(
        own_kernel,
        grid=(pairs // block,),
        in_specs=[pl.BlockSpec(memory_space=pltpu.SMEM), ids_spec(block), once(own.shape), rows, rows],
        out_specs=[out, out],
        out_shape=[jax.ShapeDtypeStruct((pairs, 2 * NH), BF)] * 2,
        compiler_params=params(),
    )(segment, ids.reshape(-1, block // 128, 128), own, low, high)


def lags_kernel(
    segment_ref, count_ref, ids_ref, rows_ref, low_ref, high_ref, low_own_ref, high_own_ref, table_ref, out_ref
):
    pairs = out_ref.shape[0]
    held = rows_ref.shape[1]
    hot = one_hot(ids_ref[0] - held, held)
    low = low_own_ref[...] + cross(hot, segment_ref, rows_ref, slice(0, 2 * NH), low_ref)
    values = jnp.dot(low, table_ref[: 2 * NH], preferred_element_type=F32)
    high = high_own_ref[...] + cross(hot, segment_ref, rows_ref, slice(2 * NH, 4 * NH), high_ref)
    values += jnp.dot(high, table_ref[2 * NH :], preferred_element_type=F32)
    place = pl.program_id(0) * pairs + lax.broadcasted_iota(jnp.int32, values.shape, 0)
    scale = 1.0 / math.sqrt(low_ref.shape[0] * NF)
    out_ref[...] = jnp.where(place < count_ref[0], values * scale, 0.0)


def lags(segment, count, ids, rows, low, high, low_own, high_own):
    segments, pairs, _ = low.shape
    block = pair_block(pairs, segments)
    table = lag_table().reshape(2, 2, NH, LAGS).transpose(1, 0, 2, 3).reshape(4 * NH, LAGS)
    bins = pl.BlockSpec((block, 2 * NH), lambda p: (p, 0))
    receivers = pl.BlockSpec((segments, block, 2 * NH), lambda p: (0, p, 0))
    in_smem = pl.BlockSpec(memory_space=pltpu.SMEM)
    return pl.pallas_call(
        lags_kernel,
        grid=(pairs // block,),
        in_specs=[in_smem, in_smem, ids_spec(block), once(rows.shape), receivers, receivers, bins, bins]
        + [whole(table.shape)],
        out_specs=pl.BlockSpec((block, LAGS), lambda p: (p, 0)),
        out_shape=jax.ShapeDtypeStruct((pairs, LAGS), F32),
        compiler_params=params(TAIL),
    )(segment, count, ids.reshape(-1, block // 128, 128), rows, low, high, low_own, high_own, table)


def on_device(strain, taps, send_rows, pair_source, pair_receiver, pair_count):
    n_tm, n_sub = lax.axis_size("tm"), lax.axis_size("sub")
    my_tm, my_half = lax.axis_index("tm"), lax.axis_index("half")
    capacity = send_rows.shape[3]
    width = strain.shape[1]
    parts = 2 if n_tm % 2 == 0 and width % 256 == 0 else 1
    held = width // parts
    order = (my_tm - jnp.arange(n_tm, dtype=jnp.int32)) % n_tm

    def shifted(array, by):
        return lax.ppermute(array, "tm", [(i, (i + by) % n_tm) for i in range(n_tm)])

    def across(array, by=0):
        pairs = [(2 * i + h, (i + by) % n_tm * 2 + 1 - h) for i in range(n_tm) for h in range(2)]
        return lax.ppermute(array, ("tm", "half"), pairs)

    def exchange(array):
        return lax.all_to_all(array, ("tm", "sub"), 0, 0, tiled=True)

    def by_segment(array):
        return array.reshape(n_tm, -1, array.shape[2])

    asked = send_rows[0].reshape(n_tm, 2, -1).transpose(1, 0, 2).reshape(1, 2, -1, 128)
    asked = jnp.broadcast_to(asked, (n_tm,) + asked.shape[1:]).reshape((2 * n_tm,) + asked.shape[2:])
    first, last, fix = edges(strain, taps)
    before = lax.ppermute(last, "tm", [(i, i + 1) for i in range(n_tm - 1)])
    after = lax.ppermute(first, "tm", [(i + 1, i) for i in range(n_tm - 1)])
    asked, first, last = lax.optimization_barrier((asked, first, last))
    asked = lax.all_to_all(asked, ("tm", "half"), 0, 0, tiled=True)
    asked = asked.reshape(n_tm, 2, -1, 128)

    dec = decimate(strain, taps)
    place = jnp.stack([my_tm, jnp.int32(n_tm)]).astype(jnp.int32)
    asked, dec = lax.optimization_barrier((asked, dec))
    asked_own = lax.dynamic_index_in_dim(asked, my_half, 1, keepdims=False)
    asked_other = lax.dynamic_index_in_dim(asked, 1 - my_half, 1, keepdims=False)

    spectra, mirrored, outgoing = [], [], []
    for p in range(parts):
        spectra.append(whiten(place, dec, first, last, before, after, fix, p * held, held))
        mirrored.append(across(spectra[p]))
        outgoing = [pick(asked_own, spectra[p], capacity, p, parts, outgoing)]
    own = exchange(outgoing[0])

    *spectra, outgoing[0] = lax.optimization_barrier((*spectra, outgoing[0]))
    receivers = []
    for a in range(n_tm):
        group = (my_tm + a) % n_tm
        each = n_tm // parts
        cut = [lax.dynamic_slice_in_dim(part, group % each * (width // n_tm), width // n_tm, 0) for part in spectra]
        rows = cut[0] if parts == 1 else jnp.where(group < each, cut[0], cut[1])
        receivers.append(shifted(rows, a) if a else rows)

    sender, column = pair_source[0] // capacity, pair_source[0] % capacity
    group, chan = sender // (2 * n_sub), sender % (2 * n_sub)
    slot = (chan % n_sub * n_tm + group) * capacity + column
    slot += jnp.where(chan // n_sub == my_half, 0, n_sub * n_tm * capacity)

    outgoing = []
    for p in range(parts):
        cost = pl.CostEstimate(flops=COST[p], bytes_accessed=COST[p] // 300, transcendentals=0)
        outgoing = [pick(asked_other, mirrored[p], capacity, p, parts, outgoing, cost)]
    outgoing, own, *receivers = lax.optimization_barrier((*outgoing, own, *receivers))
    others = exchange(outgoing)
    receiver = receive(pair_receiver[0], receivers)
    bins = cross_own(order, slot, by_segment(own), *receiver)
    return lags(order, pair_count, slot, by_segment(others), *receiver, *bins)[None]


def solution(mesh):
    n_tm, n_chan = mesh.devices.shape
    split = Mesh(mesh.devices.reshape(n_tm, 2, n_chan // 2), ("tm", "half", "sub"))
    device = ("tm", "half", "sub")
    return jax.shard_map(
        on_device,
        mesh=split,
        in_specs=(
            P("tm", ("half", "sub")),
            P(),
            P(device, None, None, None),
            P(device, None),
            P(device, None),
            P(device),
        ),
        out_specs=P(device, None, None),
        check_vma=False,
    )
```

```python
import functools
import math

import jax
import jax.numpy as jnp
import numpy as np
from jax import lax
from jax.experimental import pallas as pl
from jax.experimental.pallas import tpu as pltpu
from jax.sharding import Mesh
from jax.sharding import PartitionSpec as P

Q = 5
TAPS = 40
RIM = TAPS // 2
SEG = 1024
NF = 256
WF = 32
F0 = 40
TW = 32
WT = 64
LAGS = 256
BINS = NF + 2 * WF
TB = 128
FB = 64
RAW = 64
LEAD = 32
BAND = 384
NH = NF // 2
BF = jnp.bfloat16
F32 = jnp.float32
VMEM = 56 * 1024 * 1024
MOST = 52 * 1024 * 1024
PART = 24 * 1024 * 1024
TAIL = 59 * 1024 * 1024


def forward_table():
    phases = np.arange(F0 - WF, F0 + NF + WF)[:, None] * np.arange(SEG)[None, :] % SEG
    phases = phases * (2.0 * np.pi / SEG)
    return np.concatenate([np.cos(phases), -np.sin(phases)], axis=0).astype(BF)


def lag_table():
    phases = (F0 + np.arange(NF))[:, None] * (np.arange(LAGS) - LAGS // 2)[None, :] % SEG
    phases = phases * (2.0 * np.pi / SEG)
    return np.concatenate([np.cos(phases), -np.sin(phases)], axis=0).astype(BF)


def taper():
    bins = np.arange(NF)
    edge = np.minimum(bins, NF - 1 - bins)
    return np.where(edge < TW, 0.5 - 0.5 * np.cos(np.pi * (edge + 0.5) / TW), 1.0).astype(np.float32)


def ones_band(rows, columns, width):
    lag = np.arange(columns)[None, :] - np.arange(rows)[:, None]
    return ((lag >= 0) & (lag < width)).astype(BF)


COST = (69000000000, 69000000000)


def whole(shape):
    return pl.BlockSpec(shape, lambda *_: (0,) * len(shape))


def params(limit=VMEM):
    return pltpu.CompilerParams(vmem_limit_bytes=limit)


def fill_band(band_ref, taps_ref, work_ref, rows, shift):
    lanes = work_ref.shape[1]
    tap = lax.broadcasted_iota(jnp.int32, (8, 128), 1) - Q * lax.broadcasted_iota(jnp.int32, (8, 128), 0)
    pattern = jnp.zeros((8, 128), F32)
    for k in range(TAPS):
        pattern = jnp.where(tap == k, taps_ref[k], pattern)
    pattern = jnp.concatenate([pattern, jnp.zeros((8, lanes - 128), F32)], axis=1)
    for m in range(0, rows, 8):
        work_ref[m : m + 8] = pltpu.roll(pattern, (Q * m + shift) % lanes, 1)
    values = work_ref[:rows, : band_ref.shape[1]]
    upper = values.astype(BF)
    band_ref[:rows] = upper
    band_ref[rows:] = (values - upper.astype(F32)).astype(BF)


def filtered(band, x):
    both = jnp.dot(band, x, preferred_element_type=F32)
    rows = both.shape[0] // 2
    return (both[:rows] + both[rows:]).astype(BF)


EDGE = 352


def edge_kernel(taps_ref, x_ref, low_ref, high_ref, fix_ref, low, high, low_band, high_band, work, arrived):
    fetch_low = pltpu.make_async_copy(x_ref.at[pl.ds(0, EDGE)], low, arrived.at[0])
    fetch_high = pltpu.make_async_copy(x_ref.at[pl.ds(x_ref.shape[0] - EDGE, EDGE)], high, arrived.at[1])
    fetch_low.start()
    fetch_high.start()
    fill_band(low_band, taps_ref, work, WT, -RIM)
    fill_band(high_band, taps_ref, work, WT, EDGE - Q * WT - RIM)
    fill_band(fix_ref, taps_ref, work, 16, RAW - Q * 8 - RIM)
    fetch_low.wait()
    low_ref[:RAW] = low[:RAW]
    low_ref[RAW:] = filtered(low_band[...], low[...])
    fetch_high.wait()
    high_ref[:RAW] = high[EDGE - RAW :]
    high_ref[RAW:] = filtered(high_band[...], high[...])


def edges(x, taps):
    width = x.shape[1]
    in_vmem = pl.BlockSpec(memory_space=pltpu.VMEM)
    return pl.pallas_call(
        edge_kernel,
        in_specs=[pl.BlockSpec(memory_space=pltpu.SMEM), pl.BlockSpec(memory_space=pl.ANY)],
        out_specs=[in_vmem] * 3,
        out_shape=[
            jax.ShapeDtypeStruct((RAW + WT, width), BF),
            jax.ShapeDtypeStruct((RAW + WT, width), BF),
            jax.ShapeDtypeStruct((32, 2 * RAW), BF),
        ],
        scratch_shapes=[
            pltpu.VMEM((EDGE, width), BF),
            pltpu.VMEM((EDGE, width), BF),
            pltpu.VMEM((2 * WT, EDGE), BF),
            pltpu.VMEM((2 * WT, EDGE), BF),
            pltpu.VMEM((WT, 512), F32),
            pltpu.SemaphoreType.DMA((2,)),
        ],
        compiler_params=params(MOST),
    )(taps, x)


def decimate_kernel(taps_ref, x_ref, out_ref, x, main, first, work, arrived):
    length = out_ref.shape[0]
    fetches = arrived.shape[0]
    each = Q * length // fetches

    def fetch(k):
        rows = pl.ds(each * k, each)
        return pltpu.make_async_copy(x_ref.at[rows], x.at[rows], arrived.at[k])

    for k in range(fetches):
        fetch(k).start()
    fill_band(main, taps_ref, work, FB, LEAD - RIM)
    fill_band(first, taps_ref, work, FB, -RIM)
    here = 0
    for b in range(length // FB):
        start = max(Q * FB * b - LEAD, 0)
        stop = min(Q * FB * b - LEAD + BAND, Q * length)
        while each * here < stop:
            fetch(here).wait()
            here += 1
        band = first[...] if b == 0 else main[:, : stop - start]
        out_ref[FB * b : FB * (b + 1)] = filtered(band, x[start:stop])


def decimate(x, taps):
    rows, width = x.shape
    return pl.pallas_call(
        decimate_kernel,
        in_specs=[pl.BlockSpec(memory_space=pltpu.SMEM), pl.BlockSpec(memory_space=pl.ANY)],
        out_specs=pl.BlockSpec(memory_space=pltpu.VMEM),
        out_shape=jax.ShapeDtypeStruct((rows // Q, width), BF),
        scratch_shapes=[
            pltpu.VMEM((rows, width), BF),
            pltpu.VMEM((2 * FB, BAND), BF),
            pltpu.VMEM((2 * FB, BAND - LEAD), BF),
            pltpu.VMEM((FB, 512), F32),
            pltpu.SemaphoreType.DMA((8,)),
        ],
        compiler_params=params(MOST),
    )(taps, x)


def inverse(values):
    guess = pl.reciprocal(values, approx=True)
    return guess * (2.0 - values * guess)


def whiten_kernel(
    place_ref, dec_ref, first_ref, last_ref, before_ref, after_ref, fix_ref, ones_ref, table_ref, smooth_ref,
    taper_ref, out_ref, size, flat
):
    length = dec_ref.shape[0]
    blocks = length // TB
    place, count = place_ref[0], place_ref[1]
    low = filtered(fix_ref[...], jnp.concatenate([before_ref[:RAW], first_ref[...]])).astype(F32)
    high = filtered(fix_ref[...], jnp.concatenate([last_ref[...], after_ref[:RAW]])).astype(F32)
    before = jnp.concatenate([before_ref[RAW:].astype(F32)[:-8], low[:8]])
    after = jnp.concatenate([high[8:], after_ref[RAW:].astype(F32)[8:]])
    size[:WT] = jnp.abs(jnp.where(place > 0, before, 0.0)).astype(BF)
    size[WT + length :] = jnp.abs(jnp.where(place < count - 1, after, 0.0)).astype(BF)
    flat[...] = dec_ref[...]
    flat[:TB] = jnp.concatenate([low[8:], dec_ref[:TB].astype(F32)[8:]]).astype(BF)
    flat[length - TB :] = jnp.concatenate([dec_ref[length - TB :].astype(F32)[:-8], high[:8]]).astype(BF)
    size[WT : WT + length] = jnp.abs(flat[...])
    for b in range(blocks):
        mean = jnp.dot(ones_ref[...], size[TB * b : TB * b + TB + 2 * WT], preferred_element_type=F32)
        if b == 0 or b == blocks - 1:
            sample = place * length + TB * b + lax.broadcasted_iota(jnp.int32, (TB, 1), 0)
            total = jnp.minimum(sample + WT, count * length - 1) - jnp.maximum(sample - WT, 0) + 1
            mean = mean / total.astype(F32)
        else:
            mean = mean * (1.0 / (2 * WT + 1))
        rows = slice(TB * b, TB * (b + 1))
        flat[rows] = (flat[rows].astype(F32) * inverse(mean + 1e-05)).astype(BF)
    spectrum = jnp.dot(table_ref[...], flat[...], preferred_element_type=F32)
    real, imag = spectrum[:BINS], spectrum[BINS:]
    magnitude = jnp.sqrt(real * real + imag * imag)
    smooth = jnp.dot(smooth_ref[...], magnitude.astype(BF), preferred_element_type=F32)
    factor = taper_ref[...] * inverse(smooth * (1.0 / (2 * WF + 1)) + 1e-05)
    real, imag = real[WF : WF + NF] * factor, imag[WF : WF + NF] * factor
    out_ref[:, :NH] = real[:NH].T.astype(BF)
    out_ref[:, NH : 2 * NH] = imag[:NH].T.astype(BF)
    out_ref[:, 2 * NH : 3 * NH] = real[NH:].T.astype(BF)
    out_ref[:, 3 * NH :] = imag[NH:].T.astype(BF)


def whiten(place, dec, low, high, before, after, fix, start, held):
    length, width = dec.shape
    chunk = held
    first = start // chunk
    tables = (
        ones_band(TB, TB + 2 * WT, 2 * WT + 1),
        forward_table(),
        ones_band(NF, BINS, 2 * WF + 1),
        taper()[:, None],
    )
    column = lambda c: (0, first + c)
    return pl.pallas_call(
        whiten_kernel,
        grid=(held // chunk,),
        in_specs=[
            pl.BlockSpec(memory_space=pltpu.SMEM),
            pl.BlockSpec((length, chunk), column),
            pl.BlockSpec((RAW, chunk), column),
            pl.BlockSpec((RAW, chunk), column),
            pl.BlockSpec((RAW + WT, chunk), column),
            pl.BlockSpec((RAW + WT, chunk), column),
            whole(fix.shape),
        ]
        + [whole(table.shape) for table in tables],
        out_specs=pl.BlockSpec((chunk, 4 * NH), lambda c: (c, 0)),
        out_shape=jax.ShapeDtypeStruct((held, 4 * NH), BF),
        scratch_shapes=[pltpu.VMEM((length + 2 * WT, chunk), BF), pltpu.VMEM((length, chunk), BF)],
        compiler_params=params(VMEM),
    )(place, dec, low, high, before, after, fix, *tables)


def one_hot(ids, columns):
    wide = -(-columns // 128)
    lane = lax.broadcasted_iota(jnp.int32, (128, 128 * wide), 1)
    parts = []
    for r in range(ids.shape[0]):
        column = jnp.broadcast_to(ids[r : r + 1].astype(F32), (128, 128)).T.astype(jnp.int32)
        hits = jnp.concatenate([column] * wide, axis=1) == lane
        parts.append(jnp.where(hits, 1.0, 0.0).astype(BF)[:, :columns])
    return jnp.concatenate(parts, axis=0)


def pick_kernel(ids_ref, rows_ref, *refs):
    out_ref = refs[-1]
    owners, rows, width = out_ref.shape
    hot = one_hot(ids_ref[0], rows_ref.shape[0])
    for lane in range(0, width, 2 * NH):
        picked = jnp.dot(hot, rows_ref[:, lane : lane + 2 * NH], preferred_element_type=F32).astype(BF)
        out_ref[:, :, lane : lane + 2 * NH] = picked.reshape(owners, rows, 2 * NH)


def pick(ids, spectra, capacity, part, parts, filled, cost=None):
    groups = ids.shape[0] // parts
    owners = ids.size // ids.shape[0] // capacity
    width = spectra.shape[1]
    join = 1
    while join * capacity % 16 != 0:
        join *= 2
    steps = groups // join
    held = spectra.shape[0] // steps
    rows = owners * join * capacity
    ids = ids[part * groups : (part + 1) * groups]
    if join > 1:
        ids = ids.reshape(steps, join, owners, capacity).transpose(0, 2, 1, 3)
        ids = ids + (jnp.arange(join, dtype=jnp.int32) * (held // join))[None, None, :, None]
    return pl.pallas_call(
        pick_kernel,
        grid=(steps,),
        in_specs=[
            pl.BlockSpec((1, rows // 128, 128), lambda g: (g, 0, 0)),
            pl.BlockSpec((held, width), lambda g: (g, 0)),
        ]
        + [pl.BlockSpec(memory_space=pl.ANY) for _ in filled],
        out_specs=pl.BlockSpec((owners, join * capacity, width), lambda g: (0, part * steps + g, 0)),
        out_shape=jax.ShapeDtypeStruct((owners, parts * groups * capacity, width), BF),
        input_output_aliases={2: 0} if filled else {},
        compiler_params=params(PART),
        cost_estimate=cost,
    )(ids.reshape(steps, rows // 128, 128), spectra, *filled)


def pair_block(pairs, segments):
    return min(pairs, 512 if segments <= 4 else 128)


def ids_spec(block):
    return pl.BlockSpec((1, block // 128, 128), lambda p: (p, 0, 0))


def once(shape):
    return pl.BlockSpec(shape, lambda p: (0,) * len(shape), pipeline_mode=pl.Buffered(1))


def receive_kernel(ids_ref, *refs):
    receivers, (low_ref, high_ref) = refs[:-2], refs[-2:]
    hot = one_hot(ids_ref[0], receivers[0].shape[0])
    for k, rows in enumerate(receivers):
        low_ref[k] = jnp.dot(hot, rows[:, : 2 * NH], preferred_element_type=F32).astype(BF)
        high_ref[k] = jnp.dot(hot, rows[:, 2 * NH :], preferred_element_type=F32).astype(BF)


def receive(ids, receivers):
    segments, pairs = len(receivers), ids.size
    block = pair_block(pairs, segments)
    rows = pl.BlockSpec((segments, block, 2 * NH), lambda p: (0, p, 0))
    return pl.pallas_call(
        receive_kernel,
        grid=(pairs // block,),
        in_specs=[ids_spec(block)] + [once(r.shape) for r in receivers],
        out_specs=[rows, rows],
        out_shape=[jax.ShapeDtypeStruct((segments, pairs, 2 * NH), BF)] * 2,
        compiler_params=params(),
    )(ids.reshape(-1, block // 128, 128), *receivers)


def cross(hot, segment_ref, rows_ref, lanes, receiver_ref):
    real = imag = None
    for k in range(receiver_ref.shape[0]):
        a = jnp.dot(hot, rows_ref[segment_ref[k], :, lanes], preferred_element_type=F32)
        b = receiver_ref[k].astype(F32)
        a_re, a_im, b_re, b_im = a[:, :NH], a[:, NH:], b[:, :NH], b[:, NH:]
        re = a_re * b_re + a_im * b_im
        im = a_im * b_re - a_re * b_im
        real = re if k == 0 else real + re
        imag = im if k == 0 else imag + im
    return jnp.concatenate([real, imag], axis=1).astype(BF)


def own_kernel(segment_ref, ids_ref, own_ref, low_ref, high_ref, low_out, high_out):
    hot = one_hot(ids_ref[0], own_ref.shape[1])
    low_out[...] = cross(hot, segment_ref, own_ref, slice(0, 2 * NH), low_ref)
    high_out[...] = cross(hot, segment_ref, own_ref, slice(2 * NH, 4 * NH), high_ref)


def cross_own(segment, ids, own, low, high):
    segments, pairs, _ = low.shape
    block = pair_block(pairs, segments)
    rows = pl.BlockSpec((segments, block, 2 * NH), lambda p: (0, p, 0))
    out = pl.BlockSpec((block, 2 * NH), lambda p: (p, 0))
    return pl.pallas_call(
        own_kernel,
        grid=(pairs // block,),
        in_specs=[pl.BlockSpec(memory_space=pltpu.SMEM), ids_spec(block), once(own.shape), rows, rows],
        out_specs=[out, out],
        out_shape=[jax.ShapeDtypeStruct((pairs, 2 * NH), BF)] * 2,
        compiler_params=params(),
    )(segment, ids.reshape(-1, block // 128, 128), own, low, high)


def lags_kernel(
    segment_ref, count_ref, ids_ref, rows_ref, low_ref, high_ref, low_own_ref, high_own_ref, table_ref, out_ref
):
    pairs = out_ref.shape[0]
    held = rows_ref.shape[1]
    hot = one_hot(ids_ref[0] - held, held)
    low = low_own_ref[...] + cross(hot, segment_ref, rows_ref, slice(0, 2 * NH), low_ref)
    values = jnp.dot(low, table_ref[: 2 * NH], preferred_element_type=F32)
    high = high_own_ref[...] + cross(hot, segment_ref, rows_ref, slice(2 * NH, 4 * NH), high_ref)
    values += jnp.dot(high, table_ref[2 * NH :], preferred_element_type=F32)
    place = pl.program_id(0) * pairs + lax.broadcasted_iota(jnp.int32, values.shape, 0)
    scale = 1.0 / math.sqrt(low_ref.shape[0] * NF)
    out_ref[...] = jnp.where(place < count_ref[0], values * scale, 0.0)


def lags(segment, count, ids, rows, low, high, low_own, high_own):
    segments, pairs, _ = low.shape
    block = pair_block(pairs, segments)
    table = lag_table().reshape(2, 2, NH, LAGS).transpose(1, 0, 2, 3).reshape(4 * NH, LAGS)
    bins = pl.BlockSpec((block, 2 * NH), lambda p: (p, 0))
    receivers = pl.BlockSpec((segments, block, 2 * NH), lambda p: (0, p, 0))
    in_smem = pl.BlockSpec(memory_space=pltpu.SMEM)
    return pl.pallas_call(
        lags_kernel,
        grid=(pairs // block,),
        in_specs=[in_smem, in_smem, ids_spec(block), once(rows.shape), receivers, receivers, bins, bins]
        + [whole(table.shape)],
        out_specs=pl.BlockSpec((block, LAGS), lambda p: (p, 0)),
        out_shape=jax.ShapeDtypeStruct((pairs, LAGS), F32),
        compiler_params=params(TAIL),
    )(segment, count, ids.reshape(-1, block // 128, 128), rows, low, high, low_own, high_own, table)


def on_device(strain, taps, send_rows, pair_source, pair_receiver, pair_count):
    n_tm, n_sub = lax.axis_size("tm"), lax.axis_size("sub")
    my_tm, my_half = lax.axis_index("tm"), lax.axis_index("half")
    capacity = send_rows.shape[3]
    width = strain.shape[1]
    parts = 2 if n_tm % 2 == 0 and width % 256 == 0 else 1
    held = width // parts
    order = (my_tm - jnp.arange(n_tm, dtype=jnp.int32)) % n_tm

    def shifted(array, by):
        return lax.ppermute(array, "tm", [(i, (i + by) % n_tm) for i in range(n_tm)])

    def across(array, by=0):
        pairs = [(2 * i + h, (i + by) % n_tm * 2 + 1 - h) for i in range(n_tm) for h in range(2)]
        return lax.ppermute(array, ("tm", "half"), pairs)

    def exchange(array):
        return lax.all_to_all(array, ("tm", "sub"), 0, 0, tiled=True)

    def by_segment(array):
        return array.reshape(n_tm, -1, array.shape[2])

    asked = send_rows[0].reshape(n_tm, 2, -1).transpose(1, 0, 2).reshape(1, 2, -1, 128)
    asked = jnp.broadcast_to(asked, (n_tm,) + asked.shape[1:]).reshape((2 * n_tm,) + asked.shape[2:])
    first, last, fix = edges(strain, taps)
    before = lax.ppermute(last, "tm", [(i, i + 1) for i in range(n_tm - 1)])
    after = lax.ppermute(first, "tm", [(i + 1, i) for i in range(n_tm - 1)])
    asked, first, last = lax.optimization_barrier((asked, first, last))
    asked = lax.all_to_all(asked, ("tm", "half"), 0, 0, tiled=True)
    asked = asked.reshape(n_tm, 2, -1, 128)

    dec = decimate(strain, taps)
    place = jnp.stack([my_tm, jnp.int32(n_tm)]).astype(jnp.int32)
    asked, dec = lax.optimization_barrier((asked, dec))
    asked_own = lax.dynamic_index_in_dim(asked, my_half, 1, keepdims=False)
    asked_other = lax.dynamic_index_in_dim(asked, 1 - my_half, 1, keepdims=False)

    spectra, mirrored, outgoing = [], [], []
    for p in range(parts):
        spectra.append(whiten(place, dec, first, last, before, after, fix, p * held, held))
        outgoing = [pick(asked_own, spectra[p], capacity, p, parts, outgoing)]
        crossing = spectra[p]
        if p:
            crossing, outgoing[0] = lax.optimization_barrier((crossing, outgoing[0]))
        mirrored.append(across(crossing))
    own = exchange(outgoing[0])

    *spectra, outgoing[0] = lax.optimization_barrier((*spectra, outgoing[0]))
    receivers = []
    for a in range(n_tm):
        group = (my_tm + a) % n_tm
        each = n_tm // parts
        cut = [lax.dynamic_slice_in_dim(part, group % each * (width // n_tm), width // n_tm, 0) for part in spectra]
        rows = cut[0] if parts == 1 else jnp.where(group < each, cut[0], cut[1])
        receivers.append(shifted(rows, a) if a else rows)

    sender, column = pair_source[0] // capacity, pair_source[0] % capacity
    group, chan = sender // (2 * n_sub), sender % (2 * n_sub)
    slot = (chan % n_sub * n_tm + group) * capacity + column
    slot += jnp.where(chan // n_sub == my_half, 0, n_sub * n_tm * capacity)

    outgoing = []
    for p in range(parts):
        cost = pl.CostEstimate(flops=COST[p], bytes_accessed=COST[p] // 300, transcendentals=0)
        outgoing = [pick(asked_other, mirrored[p], capacity, p, parts, outgoing, cost)]
    outgoing, own, *receivers = lax.optimization_barrier((*outgoing, own, *receivers))
    others = exchange(outgoing)
    receiver = receive(pair_receiver[0], receivers)
    bins = cross_own(order, slot, by_segment(own), *receiver)
    return lags(order, pair_count, slot, by_segment(others), *receiver, *bins)[None]


def solution(mesh):
    n_tm, n_chan = mesh.devices.shape
    split = Mesh(mesh.devices.reshape(n_tm, 2, n_chan // 2), ("tm", "half", "sub"))
    device = ("tm", "half", "sub")
    return jax.shard_map(
        on_device,
        mesh=split,
        in_specs=(
            P("tm", ("half", "sub")),
            P(),
            P(device, None, None, None),
            P(device, None),
            P(device, None),
            P(device),
        ),
        out_specs=P(device, None, None),
        check_vma=False,
    )
```

```python
import functools
import math

import jax
import jax.numpy as jnp
import numpy as np
from jax import lax
from jax.experimental import pallas as pl
from jax.experimental.pallas import tpu as pltpu
from jax.sharding import Mesh
from jax.sharding import PartitionSpec as P

Q = 5
TAPS = 40
RIM = TAPS // 2
SEG = 1024
NF = 256
WF = 32
F0 = 40
TW = 32
WT = 64
LAGS = 256
BINS = NF + 2 * WF
TB = 128
FB = 64
RAW = 64
LEAD = 32
BAND = 384
NH = NF // 2
BF = jnp.bfloat16
F32 = jnp.float32
VMEM = 56 * 1024 * 1024
MOST = 52 * 1024 * 1024
PART = 24 * 1024 * 1024
TAIL = 59 * 1024 * 1024


def forward_table():
    phases = np.arange(F0 - WF, F0 + NF + WF)[:, None] * np.arange(SEG)[None, :] % SEG
    phases = phases * (2.0 * np.pi / SEG)
    return np.concatenate([np.cos(phases), -np.sin(phases)], axis=0).astype(BF)


def lag_table():
    phases = (F0 + np.arange(NF))[:, None] * (np.arange(LAGS) - LAGS // 2)[None, :] % SEG
    phases = phases * (2.0 * np.pi / SEG)
    return np.concatenate([np.cos(phases), -np.sin(phases)], axis=0).astype(BF)


def taper():
    bins = np.arange(NF)
    edge = np.minimum(bins, NF - 1 - bins)
    return np.where(edge < TW, 0.5 - 0.5 * np.cos(np.pi * (edge + 0.5) / TW), 1.0).astype(np.float32)


def ones_band(rows, columns, width):
    lag = np.arange(columns)[None, :] - np.arange(rows)[:, None]
    return ((lag >= 0) & (lag < width)).astype(BF)


COST = (69000000000, 69000000000)


def whole(shape):
    return pl.BlockSpec(shape, lambda *_: (0,) * len(shape))


def params(limit=VMEM):
    return pltpu.CompilerParams(vmem_limit_bytes=limit)


def fill_band(band_ref, taps_ref, work_ref, rows, shift):
    lanes = work_ref.shape[1]
    tap = lax.broadcasted_iota(jnp.int32, (8, 128), 1) - Q * lax.broadcasted_iota(jnp.int32, (8, 128), 0)
    pattern = jnp.zeros((8, 128), F32)
    for k in range(TAPS):
        pattern = jnp.where(tap == k, taps_ref[k], pattern)
    pattern = jnp.concatenate([pattern, jnp.zeros((8, lanes - 128), F32)], axis=1)
    for m in range(0, rows, 8):
        work_ref[m : m + 8] = pltpu.roll(pattern, (Q * m + shift) % lanes, 1)
    values = work_ref[:rows, : band_ref.shape[1]]
    upper = values.astype(BF)
    band_ref[:rows] = upper
    band_ref[rows:] = (values - upper.astype(F32)).astype(BF)


def filtered(band, x):
    both = jnp.dot(band, x, preferred_element_type=F32)
    rows = both.shape[0] // 2
    return (both[:rows] + both[rows:]).astype(BF)


EDGE = 352


def edge_kernel(taps_ref, x_ref, low_ref, high_ref, fix_ref, low, high, low_band, high_band, work, arrived):
    fetch_low = pltpu.make_async_copy(x_ref.at[pl.ds(0, EDGE)], low, arrived.at[0])
    fetch_high = pltpu.make_async_copy(x_ref.at[pl.ds(x_ref.shape[0] - EDGE, EDGE)], high, arrived.at[1])
    fetch_low.start()
    fetch_high.start()
    fill_band(low_band, taps_ref, work, WT, -RIM)
    fill_band(high_band, taps_ref, work, WT, EDGE - Q * WT - RIM)
    fill_band(fix_ref, taps_ref, work, 16, RAW - Q * 8 - RIM)
    fetch_low.wait()
    low_ref[:RAW] = low[:RAW]
    low_ref[RAW:] = filtered(low_band[...], low[...])
    fetch_high.wait()
    high_ref[:RAW] = high[EDGE - RAW :]
    high_ref[RAW:] = filtered(high_band[...], high[...])


def edges(x, taps):
    width = x.shape[1]
    in_vmem = pl.BlockSpec(memory_space=pltpu.VMEM)
    return pl.pallas_call(
        edge_kernel,
        in_specs=[pl.BlockSpec(memory_space=pltpu.SMEM), pl.BlockSpec(memory_space=pl.ANY)],
        out_specs=[in_vmem] * 3,
        out_shape=[
            jax.ShapeDtypeStruct((RAW + WT, width), BF),
            jax.ShapeDtypeStruct((RAW + WT, width), BF),
            jax.ShapeDtypeStruct((32, 2 * RAW), BF),
        ],
        scratch_shapes=[
            pltpu.VMEM((EDGE, width), BF),
            pltpu.VMEM((EDGE, width), BF),
            pltpu.VMEM((2 * WT, EDGE), BF),
            pltpu.VMEM((2 * WT, EDGE), BF),
            pltpu.VMEM((WT, 512), F32),
            pltpu.SemaphoreType.DMA((2,)),
        ],
        compiler_params=params(MOST),
    )(taps, x)


def decimate_kernel(taps_ref, x_ref, out_ref, x, main, first, work, arrived):
    length = out_ref.shape[0]
    fetches = arrived.shape[0]
    each = Q * length // fetches

    def fetch(k):
        rows = pl.ds(each * k, each)
        return pltpu.make_async_copy(x_ref.at[rows], x.at[rows], arrived.at[k])

    for k in range(fetches):
        fetch(k).start()
    fill_band(main, taps_ref, work, FB, LEAD - RIM)
    fill_band(first, taps_ref, work, FB, -RIM)
    here = 0
    for b in range(length // FB):
        start = max(Q * FB * b - LEAD, 0)
        stop = min(Q * FB * b - LEAD + BAND, Q * length)
        while each * here < stop:
            fetch(here).wait()
            here += 1
        band = first[...] if b == 0 else main[:, : stop - start]
        out_ref[FB * b : FB * (b + 1)] = filtered(band, x[start:stop])


def decimate(x, taps):
    rows, width = x.shape
    return pl.pallas_call(
        decimate_kernel,
        in_specs=[pl.BlockSpec(memory_space=pltpu.SMEM), pl.BlockSpec(memory_space=pl.ANY)],
        out_specs=pl.BlockSpec(memory_space=pltpu.VMEM),
        out_shape=jax.ShapeDtypeStruct((rows // Q, width), BF),
        scratch_shapes=[
            pltpu.VMEM((rows, width), BF),
            pltpu.VMEM((2 * FB, BAND), BF),
            pltpu.VMEM((2 * FB, BAND - LEAD), BF),
            pltpu.VMEM((FB, 512), F32),
            pltpu.SemaphoreType.DMA((8,)),
        ],
        compiler_params=params(MOST),
    )(taps, x)


def inverse(values):
    guess = pl.reciprocal(values, approx=True)
    return guess * (2.0 - values * guess)


def whiten_kernel(
    place_ref, dec_ref, first_ref, last_ref, before_ref, after_ref, fix_ref, ones_ref, table_ref, smooth_ref,
    taper_ref, out_ref, size, flat
):
    length = dec_ref.shape[0]
    blocks = length // TB
    place, count = place_ref[0], place_ref[1]
    low = filtered(fix_ref[...], jnp.concatenate([before_ref[:RAW], first_ref[...]])).astype(F32)
    high = filtered(fix_ref[...], jnp.concatenate([last_ref[...], after_ref[:RAW]])).astype(F32)
    before = jnp.concatenate([before_ref[RAW:].astype(F32)[:-8], low[:8]])
    after = jnp.concatenate([high[8:], after_ref[RAW:].astype(F32)[8:]])
    size[:WT] = jnp.abs(jnp.where(place > 0, before, 0.0)).astype(BF)
    size[WT + length :] = jnp.abs(jnp.where(place < count - 1, after, 0.0)).astype(BF)
    flat[...] = dec_ref[...]
    flat[:TB] = jnp.concatenate([low[8:], dec_ref[:TB].astype(F32)[8:]]).astype(BF)
    flat[length - TB :] = jnp.concatenate([dec_ref[length - TB :].astype(F32)[:-8], high[:8]]).astype(BF)
    size[WT : WT + length] = jnp.abs(flat[...])
    for b in range(blocks):
        mean = jnp.dot(ones_ref[...], size[TB * b : TB * b + TB + 2 * WT], preferred_element_type=F32)
        if b == 0 or b == blocks - 1:
            sample = place * length + TB * b + lax.broadcasted_iota(jnp.int32, (TB, 1), 0)
            total = jnp.minimum(sample + WT, count * length - 1) - jnp.maximum(sample - WT, 0) + 1
            mean = mean / total.astype(F32)
        else:
            mean = mean * (1.0 / (2 * WT + 1))
        rows = slice(TB * b, TB * (b + 1))
        flat[rows] = (flat[rows].astype(F32) * inverse(mean + 1e-05)).astype(BF)
    spectrum = jnp.dot(table_ref[...], flat[...], preferred_element_type=F32)
    real, imag = spectrum[:BINS], spectrum[BINS:]
    magnitude = jnp.sqrt(real * real + imag * imag)
    smooth = jnp.dot(smooth_ref[...], magnitude.astype(BF), preferred_element_type=F32)
    factor = taper_ref[...] * inverse(smooth * (1.0 / (2 * WF + 1)) + 1e-05)
    real, imag = real[WF : WF + NF] * factor, imag[WF : WF + NF] * factor
    out_ref[:, :NH] = real[:NH].T.astype(BF)
    out_ref[:, NH : 2 * NH] = imag[:NH].T.astype(BF)
    out_ref[:, 2 * NH : 3 * NH] = real[NH:].T.astype(BF)
    out_ref[:, 3 * NH :] = imag[NH:].T.astype(BF)


def whiten(place, dec, low, high, before, after, fix, start, held):
    length, width = dec.shape
    chunk = held
    first = start // chunk
    tables = (
        ones_band(TB, TB + 2 * WT, 2 * WT + 1),
        forward_table(),
        ones_band(NF, BINS, 2 * WF + 1),
        taper()[:, None],
    )
    column = lambda c: (0, first + c)
    return pl.pallas_call(
        whiten_kernel,
        grid=(held // chunk,),
        in_specs=[
            pl.BlockSpec(memory_space=pltpu.SMEM),
            pl.BlockSpec((length, chunk), column),
            pl.BlockSpec((RAW, chunk), column),
            pl.BlockSpec((RAW, chunk), column),
            pl.BlockSpec((RAW + WT, chunk), column),
            pl.BlockSpec((RAW + WT, chunk), column),
            whole(fix.shape),
        ]
        + [whole(table.shape) for table in tables],
        out_specs=pl.BlockSpec((chunk, 4 * NH), lambda c: (c, 0)),
        out_shape=jax.ShapeDtypeStruct((held, 4 * NH), BF),
        scratch_shapes=[pltpu.VMEM((length + 2 * WT, chunk), BF), pltpu.VMEM((length, chunk), BF)],
        compiler_params=params(VMEM),
    )(place, dec, low, high, before, after, fix, *tables)


def one_hot(ids, columns):
    wide = -(-columns // 128)
    lane = lax.broadcasted_iota(jnp.int32, (128, 128 * wide), 1)
    parts = []
    for r in range(ids.shape[0]):
        column = jnp.broadcast_to(ids[r : r + 1].astype(F32), (128, 128)).T.astype(jnp.int32)
        hits = jnp.concatenate([column] * wide, axis=1) == lane
        parts.append(jnp.where(hits, 1.0, 0.0).astype(BF)[:, :columns])
    return jnp.concatenate(parts, axis=0)


def pick_kernel(ids_ref, rows_ref, *refs):
    out_ref = refs[-1]
    owners, rows, width = out_ref.shape
    hot = one_hot(ids_ref[0], rows_ref.shape[0])
    for lane in range(0, width, 2 * NH):
        picked = jnp.dot(hot, rows_ref[:, lane : lane + 2 * NH], preferred_element_type=F32).astype(BF)
        out_ref[:, :, lane : lane + 2 * NH] = picked.reshape(owners, rows, 2 * NH)


def pick(ids, spectra, capacity, part, parts, filled, cost=None):
    groups = ids.shape[0] // parts
    owners = ids.size // ids.shape[0] // capacity
    width = spectra.shape[1]
    join = 1
    while join * capacity % 16 != 0:
        join *= 2
    steps = groups // join
    held = spectra.shape[0] // steps
    rows = owners * join * capacity
    ids = ids[part * groups : (part + 1) * groups]
    if join > 1:
        ids = ids.reshape(steps, join, owners, capacity).transpose(0, 2, 1, 3)
        ids = ids + (jnp.arange(join, dtype=jnp.int32) * (held // join))[None, None, :, None]
    return pl.pallas_call(
        pick_kernel,
        grid=(steps,),
        in_specs=[
            pl.BlockSpec((1, rows // 128, 128), lambda g: (g, 0, 0)),
            pl.BlockSpec((held, width), lambda g: (g, 0)),
        ]
        + [pl.BlockSpec(memory_space=pl.ANY) for _ in filled],
        out_specs=pl.BlockSpec((owners, join * capacity, width), lambda g: (0, part * steps + g, 0)),
        out_shape=jax.ShapeDtypeStruct((owners, parts * groups * capacity, width), BF),
        input_output_aliases={2: 0} if filled else {},
        compiler_params=params(PART),
        cost_estimate=cost,
    )(ids.reshape(steps, rows // 128, 128), spectra, *filled)


def pair_block(pairs, segments):
    return min(pairs, 512 if segments <= 4 else 128)


def ids_spec(block):
    return pl.BlockSpec((1, block // 128, 128), lambda p: (p, 0, 0))


def once(shape):
    return pl.BlockSpec(shape, lambda p: (0,) * len(shape), pipeline_mode=pl.Buffered(1))


def receive_kernel(ids_ref, *refs):
    receivers, (low_ref, high_ref) = refs[:-2], refs[-2:]
    hot = one_hot(ids_ref[0], receivers[0].shape[0])
    for k, rows in enumerate(receivers):
        low_ref[k] = jnp.dot(hot, rows[:, : 2 * NH], preferred_element_type=F32).astype(BF)
        high_ref[k] = jnp.dot(hot, rows[:, 2 * NH :], preferred_element_type=F32).astype(BF)


def receive(ids, receivers):
    segments, pairs = len(receivers), ids.size
    block = pair_block(pairs, segments)
    rows = pl.BlockSpec((segments, block, 2 * NH), lambda p: (0, p, 0))
    return pl.pallas_call(
        receive_kernel,
        grid=(pairs // block,),
        in_specs=[ids_spec(block)] + [once(r.shape) for r in receivers],
        out_specs=[rows, rows],
        out_shape=[jax.ShapeDtypeStruct((segments, pairs, 2 * NH), BF)] * 2,
        compiler_params=params(),
    )(ids.reshape(-1, block // 128, 128), *receivers)


def cross(hot, segment_ref, rows_ref, lanes, receiver_ref):
    real = imag = None
    for k in range(receiver_ref.shape[0]):
        a = jnp.dot(hot, rows_ref[segment_ref[k], :, lanes], preferred_element_type=F32)
        b = receiver_ref[k].astype(F32)
        a_re, a_im, b_re, b_im = a[:, :NH], a[:, NH:], b[:, :NH], b[:, NH:]
        re = a_re * b_re + a_im * b_im
        im = a_im * b_re - a_re * b_im
        real = re if k == 0 else real + re
        imag = im if k == 0 else imag + im
    return jnp.concatenate([real, imag], axis=1).astype(BF)


def own_kernel(segment_ref, ids_ref, own_ref, low_ref, high_ref, low_out, high_out):
    hot = one_hot(ids_ref[0], own_ref.shape[1])
    low_out[...] = cross(hot, segment_ref, own_ref, slice(0, 2 * NH), low_ref)
    high_out[...] = cross(hot, segment_ref, own_ref, slice(2 * NH, 4 * NH), high_ref)


def cross_own(segment, ids, own, low, high):
    segments, pairs, _ = low.shape
    block = pair_block(pairs, segments)
    rows = pl.BlockSpec((segments, block, 2 * NH), lambda p: (0, p, 0))
    out = pl.BlockSpec((block, 2 * NH), lambda p: (p, 0))
    return pl.pallas_call(
        own_kernel,
        grid=(pairs // block,),
        in_specs=[pl.BlockSpec(memory_space=pltpu.SMEM), ids_spec(block), once(own.shape), rows, rows],
        out_specs=[out, out],
        out_shape=[jax.ShapeDtypeStruct((pairs, 2 * NH), BF)] * 2,
        compiler_params=params(),
    )(segment, ids.reshape(-1, block // 128, 128), own, low, high)


def lags_kernel(
    segment_ref, count_ref, ids_ref, given_ref, low_ref, high_ref, low_own_ref, high_own_ref, table_ref, out_ref,
    rows_ref, arrived
):
    pairs = out_ref.shape[0]
    held = rows_ref.shape[1]
    hot = one_hot(ids_ref[0] - held, held)

    @pl.when(pl.program_id(0) == 0)
    def _():
        fetch = pltpu.make_async_copy(given_ref, rows_ref, arrived)
        fetch.start()
        fetch.wait()

    low = low_own_ref[...] + cross(hot, segment_ref, rows_ref, slice(0, 2 * NH), low_ref)
    values = jnp.dot(low, table_ref[: 2 * NH], preferred_element_type=F32)
    high = high_own_ref[...] + cross(hot, segment_ref, rows_ref, slice(2 * NH, 4 * NH), high_ref)
    values += jnp.dot(high, table_ref[2 * NH :], preferred_element_type=F32)
    place = pl.program_id(0) * pairs + lax.broadcasted_iota(jnp.int32, values.shape, 0)
    scale = 1.0 / math.sqrt(low_ref.shape[0] * NF)
    out_ref[...] = jnp.where(place < count_ref[0], values * scale, 0.0)


def lags(segment, count, ids, rows, low, high, low_own, high_own):
    segments, pairs, _ = low.shape
    block = pair_block(pairs, segments)
    table = lag_table().reshape(2, 2, NH, LAGS).transpose(1, 0, 2, 3).reshape(4 * NH, LAGS)
    bins = pl.BlockSpec((block, 2 * NH), lambda p: (p, 0))
    receivers = pl.BlockSpec((segments, block, 2 * NH), lambda p: (0, p, 0))
    in_smem = pl.BlockSpec(memory_space=pltpu.SMEM)
    return pl.pallas_call(
        lags_kernel,
        grid=(pairs // block,),
        in_specs=[in_smem, in_smem, ids_spec(block), pl.BlockSpec(memory_space=pl.ANY), receivers, receivers, bins, bins]
        + [whole(table.shape)],
        out_specs=pl.BlockSpec((block, LAGS), lambda p: (p, 0)),
        out_shape=jax.ShapeDtypeStruct((pairs, LAGS), F32),
        scratch_shapes=[pltpu.VMEM(rows.shape, BF), pltpu.SemaphoreType.DMA],
        compiler_params=params(TAIL),
    )(segment, count, ids.reshape(-1, block // 128, 128), rows, low, high, low_own, high_own, table)


def on_device(strain, taps, send_rows, pair_source, pair_receiver, pair_count):
    n_tm, n_sub = lax.axis_size("tm"), lax.axis_size("sub")
    my_tm, my_half = lax.axis_index("tm"), lax.axis_index("half")
    capacity = send_rows.shape[3]
    width = strain.shape[1]
    parts = 2 if n_tm % 2 == 0 and width % 256 == 0 else 1
    held = width // parts
    order = (my_tm - jnp.arange(n_tm, dtype=jnp.int32)) % n_tm

    def shifted(array, by):
        return lax.ppermute(array, "tm", [(i, (i + by) % n_tm) for i in range(n_tm)])

    def across(array, by=0):
        pairs = [(2 * i + h, (i + by) % n_tm * 2 + 1 - h) for i in range(n_tm) for h in range(2)]
        return lax.ppermute(array, ("tm", "half"), pairs)

    def exchange(array):
        return lax.all_to_all(array, ("tm", "sub"), 0, 0, tiled=True)

    def by_segment(array):
        return array.reshape(n_tm, -1, array.shape[2])

    asked = send_rows[0].reshape(n_tm, 2, -1).transpose(1, 0, 2).reshape(1, 2, -1, 128)
    asked = jnp.broadcast_to(asked, (n_tm,) + asked.shape[1:]).reshape((2 * n_tm,) + asked.shape[2:])
    first, last, fix = edges(strain, taps)
    before = lax.ppermute(last, "tm", [(i, i + 1) for i in range(n_tm - 1)])
    after = lax.ppermute(first, "tm", [(i + 1, i) for i in range(n_tm - 1)])
    asked, first, last = lax.optimization_barrier((asked, first, last))
    asked = lax.all_to_all(asked, ("tm", "half"), 0, 0, tiled=True)
    asked = asked.reshape(n_tm, 2, -1, 128)

    dec = decimate(strain, taps)
    place = jnp.stack([my_tm, jnp.int32(n_tm)]).astype(jnp.int32)
    asked, dec = lax.optimization_barrier((asked, dec))
    asked_own = lax.dynamic_index_in_dim(asked, my_half, 1, keepdims=False)
    asked_other = lax.dynamic_index_in_dim(asked, 1 - my_half, 1, keepdims=False)

    spectra, mirrored, outgoing = [], [], []
    for p in range(parts):
        spectra.append(whiten(place, dec, first, last, before, after, fix, p * held, held))
        outgoing = [pick(asked_own, spectra[p], capacity, p, parts, outgoing)]
        crossing = spectra[p]
        if p:
            crossing, outgoing[0] = lax.optimization_barrier((crossing, outgoing[0]))
        mirrored.append(across(crossing))
    own = exchange(outgoing[0])

    *spectra, outgoing[0] = lax.optimization_barrier((*spectra, outgoing[0]))
    receivers = []
    for a in range(n_tm):
        group = (my_tm + a) % n_tm
        each = n_tm // parts
        cut = [lax.dynamic_slice_in_dim(part, group % each * (width // n_tm), width // n_tm, 0) for part in spectra]
        rows = cut[0] if parts == 1 else jnp.where(group < each, cut[0], cut[1])
        receivers.append(shifted(rows, a) if a else rows)

    sender, column = pair_source[0] // capacity, pair_source[0] % capacity
    group, chan = sender // (2 * n_sub), sender % (2 * n_sub)
    slot = (chan % n_sub * n_tm + group) * capacity + column
    slot += jnp.where(chan // n_sub == my_half, 0, n_sub * n_tm * capacity)

    outgoing = []
    for p in range(parts):
        cost = pl.CostEstimate(flops=COST[p], bytes_accessed=COST[p] // 300, transcendentals=0)
        outgoing = [pick(asked_other, mirrored[p], capacity, p, parts, outgoing, cost)]
    outgoing, own, *receivers = lax.optimization_barrier((*outgoing, own, *receivers))
    others = exchange(outgoing)
    receiver = receive(pair_receiver[0], receivers)
    bins = cross_own(order, slot, by_segment(own), *receiver)
    return lags(order, pair_count, slot, by_segment(others), *receiver, *bins)[None]


def solution(mesh):
    n_tm, n_chan = mesh.devices.shape
    split = Mesh(mesh.devices.reshape(n_tm, 2, n_chan // 2), ("tm", "half", "sub"))
    device = ("tm", "half", "sub")
    return jax.shard_map(
        on_device,
        mesh=split,
        in_specs=(
            P("tm", ("half", "sub")),
            P(),
            P(device, None, None, None),
            P(device, None),
            P(device, None),
            P(device),
        ),
        out_specs=P(device, None, None),
        check_vma=False,
    )
```
